128 devices in a mesh: seq: 8 (over y, core), head: 16 (over z, x).
Axes of the slice: x: 4, y: 4, z: 4, core: 2. Of those that a mesh axis runs over, the one named last changes fastest.
Arguments:
- tokens: bfloat16 [6144, 8192], P('seq', 'head'), may hold values from -6 to 6
- w_query: bfloat16 [8192, 8192], P(None, 'head'), may hold values from -0.0625 to 0.0625
- w_key: bfloat16 [8192, 1024], P(None, 'head'), may hold values from -0.0625 to 0.0625
- w_value: bfloat16 [8192, 1024], P(None, 'head'), may hold values from -0.0625 to 0.0625
- map_query: float32 [64, 128, 64], P('head'), may hold values from -0.5 to 0.5
- map_key: float32 [64, 128, 64], P('head'), may hold values from -0.5 to 0.5
Outputs:
- student_out: bfloat16 [6144, 8192], P('seq', 'head')
- grad_query_map: float32 [64, 128, 64], P('head')
- grad_key_map: float32 [64, 128, 64], P('head')
The draws below stay inside these ranges and needn't reach their ends.
All inputs are finite; a program needn't handle non-finite values.
Results may differ from the reference program's by a relative error of at most 0.013.
Values may be sent and summed in bfloat16 or wider, within the bound.
No kernel may reach another device: no remote copies, remote signals or barrier semaphores. Data moves between devices by JAX's collectives and lax.ppermute only.
A program may use at most 128 MiB of HBM per device.

```python
import math
import jax
import jax.numpy as jnp
from jax import lax

D = 8192
HEADS = 64
KVH = 8
DH = 128
FEAT = 64
TOKENS = 6144


def block_levels(rng, shape, shards, smallest, largest):
    factor_of = 1.0
    for position, blocks in shards:
        heights = jax.random.uniform(jax.random.fold_in(jax.random.fold_in(rng, 6), position), (blocks,), jnp.float32, smallest / len(shards), largest / len(shards))
        factor_of = factor_of * jnp.repeat(jnp.exp(heights), shape[position] // blocks).reshape((-1,) + (1,) * (len(shape) - 1 - position))
    return factor_of


def gaussian(key, dims, deviation, limit, shards=(), held_as=jnp.bfloat16):
    loudness = block_levels(key, dims, shards, -0.22, 0.18) if shards else 1.0
    entries = jax.random.normal(key, dims, jnp.float32) * deviation * loudness
    return jnp.minimum(jnp.maximum(entries, -limit), limit).astype(held_as)


def setup_inputs(seed: int = 0) -> dict:
    seeds = jax.random.split(jax.random.key(seed), 7)
    tokens = gaussian(seeds[0], (TOKENS, D), 1.0, 6.0, ((0, 8), (1, 16)))
    w_query = gaussian(seeds[1], (D, HEADS * DH), D ** -0.5, 0.0625, ((1, 16),))
    w_key = gaussian(seeds[2], (D, KVH * DH), D ** -0.5, 0.0625, ((1, 16),))
    w_value = gaussian(seeds[3], (D, KVH * DH), D ** -0.5, 0.0625, ((1, 16),))
    map_query = gaussian(seeds[4], (HEADS, DH, FEAT), DH ** -0.5, 0.5, ((0, 16),), jnp.float32)
    map_key = gaussian(seeds[5], (HEADS, DH, FEAT), DH ** -0.5, 0.5, ((0, 16),), jnp.float32)
    return dict(tokens=tokens, w_query=w_query, w_key=w_key, w_value=w_value, map_query=map_query, map_key=map_key)


ROPE_BASE = 500000.0
MATMUL_ACCURACY = lax.Precision.HIGHEST

def rope_tables(length, width, offset):
    half_width = width // 2
    positions = (offset + jnp.arange(length)).astype(jnp.float32)
    exponent = jnp.arange(half_width).astype(jnp.float32) * (2.0 / width)
    frequency = jnp.power(jnp.float32(ROPE_BASE), -exponent)
    angles = positions[:, None] * frequency[None, :]
    return (jnp.cos(angles), jnp.sin(angles))

def rotate(vectors, cosine, sine):
    half_width = vectors.shape[-1] // 2
    first = vectors[..., :half_width]
    second = vectors[..., half_width:]
    cosine = cosine[:, None, :]
    sine = sine[:, None, :]
    return jnp.concatenate([first * cosine - second * sine, second * cosine + first * sine], axis=-1)

def feature_map(vectors, weights):
    logits = jnp.einsum('thd,hdf->thf', vectors, weights, precision=MATMUL_ACCURACY)
    upper = jnp.exp(logits)
    lower = jnp.exp(-logits)
    return jnp.concatenate([upper / lax.optimization_barrier(jnp.sum(upper, -1, keepdims=True)), lower / lax.optimization_barrier(jnp.sum(lower, -1, keepdims=True))], axis=-1)

def reference(tokens, w_query, w_key, w_value, map_query, map_key):
    length = tokens.shape[0]
    group = HEADS // KVH
    query_rows = jnp.dot(tokens, w_query, preferred_element_type=jnp.float32).reshape(length, HEADS, DH)
    keys = jnp.dot(tokens, w_key, preferred_element_type=jnp.float32).astype(jnp.bfloat16)
    values = jnp.dot(tokens, w_value, preferred_element_type=jnp.float32).astype(jnp.bfloat16)
    cosine, sine = rope_tables(length, DH, 0)
    queries_rot = rotate(query_rows, cosine, sine).astype(jnp.bfloat16)
    keys_rot = rotate(keys.astype(jnp.float32).reshape(length, KVH, DH), cosine, sine).astype(jnp.bfloat16)
    values = values.reshape(length, KVH, DH)
    causal = jnp.arange(length)[None, :] <= jnp.arange(length)[:, None]
    query_head_count = jnp.transpose(queries_rot, (1, 0, 2))
    key_heads = jnp.transpose(keys_rot, (1, 0, 2))
    value_heads = jnp.transpose(values, (1, 0, 2))
    scale = 1.0 / math.sqrt(DH)

    def teacher_head(index):
        shared_index = index // group
        scores = jnp.dot(query_head_count[index], key_heads[shared_index].T, preferred_element_type=jnp.float32) * scale
        weights = jnp.exp(jnp.where(causal, scores, -1e+30))
        total = lax.optimization_barrier(jnp.sum(weights, -1))
        mixed = jnp.dot(weights.astype(jnp.bfloat16), value_heads[shared_index], preferred_element_type=jnp.float32)
        return (mixed / total[:, None]).astype(jnp.bfloat16)
    teacher = lax.map(teacher_head, jnp.arange(HEADS))
    target = jnp.transpose(teacher, (1, 0, 2)).astype(jnp.float32)
    keys_wide = jnp.repeat(keys_rot.astype(jnp.float32), group, axis=1)
    value_rows_broad = jnp.transpose(jnp.repeat(values.astype(jnp.float32), group, axis=1), (1, 0, 2))
    query_float = queries_rot.astype(jnp.float32)
    mask = causal.astype(jnp.float32)

    def student_head(inputs):
        query_feature_rows, key_feature_rows, head_values = inputs
        within = jnp.dot(query_feature_rows, key_feature_rows.T, precision=MATMUL_ACCURACY) * mask
        numerator = jnp.dot(within, head_values, precision=MATMUL_ACCURACY)
        return numerator / lax.optimization_barrier(jnp.sum(within, -1))[:, None]

    def student(query_weights, key_weights):
        query_features = jnp.transpose(feature_map(query_float, query_weights), (1, 0, 2))
        key_features = jnp.transpose(feature_map(keys_wide, key_weights), (1, 0, 2))
        outputs = lax.map(jax.checkpoint(student_head), (query_features, key_features, value_rows_broad))
        outputs = jnp.transpose(outputs, (1, 0, 2))
        loss = jnp.sum((outputs - target) ** 2)
        return (loss, outputs)
    loss, pullback, outputs = jax.vjp(student, map_query, map_key, has_aux=True)
    grad_query_map, grad_key_map = pullback(jnp.ones_like(loss))
    student_out = outputs.astype(jnp.bfloat16).reshape(length, HEADS * DH)
    return (student_out, grad_query_map, grad_key_map)
```

```python
import math

import jax
import jax.numpy as jnp
from jax import lax
from jax.experimental import pallas as pl
from jax.experimental.pallas import tpu as pltpu
from jax.sharding import PartitionSpec as P

DH = 128
ROPE_BASE = 500000.0
NT = (((1,), (1,)), ((), ()))
TN = (((0,), (0,)), ((), ()))
F32 = jnp.float32
BF16 = jnp.bfloat16


def partner(value, axis, apart):
    mask = 2**apart
    pairs = [(source, source ^ mask) for source in range(lax.axis_size(axis))]
    return lax.ppermute(value, axis, pairs)


def rope_tables(length, width, offset):
    half_width = width // 2
    positions = (offset + jnp.arange(length)).astype(F32)
    exponent = jnp.arange(half_width).astype(F32) * (2.0 / width)
    frequency = jnp.power(jnp.float32(ROPE_BASE), -exponent)
    angles = positions[:, None] * frequency[None, :]
    cosine, sine = jnp.cos(angles), jnp.sin(angles)
    return jnp.concatenate([cosine, cosine], 1), jnp.concatenate([-sine, sine], 1)


def dot(a, b, dims=None):
    if dims is None:
        return jnp.dot(a, b, preferred_element_type=F32)
    return lax.dot_general(a, b, dims, preferred_element_type=F32)


def project_kernel(x_ref, wq_ref, wkv_ref, cos_ref, sin_ref, q_ref, kv_ref, acc_q, acc_kv):
    step = pl.program_id(0)
    x = x_ref[0]
    pq = dot(x, wq_ref[...])
    pkv = dot(x, wkv_ref[...])

    @pl.when(step == 0)
    def _():
        acc_q[...] = pq
        acc_kv[...] = pkv

    @pl.when(step > 0)
    def _():
        acc_q[...] += pq
        acc_kv[...] += pkv

    @pl.when(step == pl.num_programs(0) - 1)
    def _():
        cosine = cos_ref[...]
        sine = sin_ref[...]

        def turn(u):
            return (u * cosine + pltpu.roll(u, DH // 2, 1) * sine).astype(BF16)

        for h in range(q_ref.shape[1] // DH):
            q_ref[:, h * DH : (h + 1) * DH] = turn(acc_q[:, h * DH : (h + 1) * DH])
        keys = acc_kv[:, :DH].astype(BF16).astype(F32)
        kv_ref[:, :DH] = turn(keys)
        kv_ref[:, DH:] = acc_kv[:, DH:].astype(BF16)


def project(gathered, w_query, w_kv, cosine, sine):
    parts, rows, depth = gathered.shape
    nq = w_query.shape[1]
    return pl.pallas_call(
        project_kernel,
        grid=(parts,),
        in_specs=[
            pl.BlockSpec((1, rows, depth), lambda k: (k, 0, 0)),
            pl.BlockSpec((depth, nq), lambda k: (k, 0)),
            pl.BlockSpec((depth, 2 * DH), lambda k: (k, 0)),
            pl.BlockSpec((rows, DH), lambda k: (0, 0)),
            pl.BlockSpec((rows, DH), lambda k: (0, 0)),
        ],
        out_specs=[
            pl.BlockSpec((rows, nq), lambda k: (0, 0)),
            pl.BlockSpec((rows, 2 * DH), lambda k: (0, 0)),
        ],
        out_shape=[
            jax.ShapeDtypeStruct((rows, nq), BF16),
            jax.ShapeDtypeStruct((rows, 2 * DH), BF16),
        ],
        scratch_shapes=[pltpu.VMEM((rows, nq), F32), pltpu.VMEM((rows, 2 * DH), F32)],
        compiler_params=pltpu.CompilerParams(vmem_limit_bytes=48 * 2**20),
        name="project",
    )(gathered, w_query, w_kv, cosine, sine)


def attention_kernel(
    chain_ref, q_ref, kv_ref, mq_ref, mk_ref,
    out_ref, gq_ref, gk_ref,
    wq_s, wk_s, kf_s, qf_s, acc_s, state_s, dstate_s, kt_s, gk_s,
    *, rows, heads, chunk,
):
    me = chain_ref[0]
    half = DH // 2
    fold = math.log2(math.e) / math.sqrt(DH)
    log2e = math.log2(math.e)

    i0 = lax.broadcasted_iota(jnp.int32, (2 * DH, 2 * DH), 0) // half
    i1 = lax.broadcasted_iota(jnp.int32, (2 * DH, 2 * DH), 1) // half
    halves = (i0 == i1).astype(F32).astype(BF16)

    def half_sums(u):
        width = u.shape[1]
        return jnp.concatenate(
            [dot(u[:, c : c + 2 * DH], halves) for c in range(0, width, 2 * DH)], 1
        )

    for h in range(heads):
        for src, dst in ((mq_ref, wq_s), (mk_ref, wk_s)):
            w = src[h] * log2e
            w = jnp.concatenate([w, -w], 1)
            high = w.astype(BF16)
            dst[:DH, h * DH : (h + 1) * DH] = high
            dst[DH:, h * DH : (h + 1) * DH] = (w - high.astype(F32)).astype(BF16)

    acc_s[...] = jnp.zeros_like(acc_s)
    state_s[...] = jnp.zeros_like(state_s)
    gk_s[...] = jnp.zeros_like(gk_s)
    ones = jnp.ones((chunk, DH), BF16)

    def key_features(first):
        k = kv_ref[pl.ds(first, chunk), :DH]
        e = jnp.exp2(dot(jnp.concatenate([k, k], 1), wk_s[...]))
        f = (e / half_sums(e.astype(BF16))).astype(BF16)
        kf_s[pl.ds(first, chunk), :] = f
        return f

    def values_wide(first):
        return jnp.concatenate([kv_ref[pl.ds(first, chunk), DH:], ones], 1)

    def teacher(first, tile, size, masked):
        k = kv_ref[pl.ds(first, chunk), :DH]
        va = values_wide(first)
        for h in range(heads):
            q = q_ref[tile * size : (tile + 1) * size, h * DH : (h + 1) * DH]
            p = jnp.exp2(dot(q, k, NT) * fold)
            if masked is not None:
                p = jnp.where(masked, p, 0.0)
            acc_s[h, tile * size : (tile + 1) * size, :] += dot(p.astype(BF16), va)

    def earlier(c, carry):
        first = pl.multiple_of(c * chunk, chunk)
        f = key_features(first)
        va = values_wide(first)
        state_s[...] += dot(va, f, TN)
        for tile in range(rows // chunk):
            teacher(first, tile, chunk, None)
        return carry

    tiles = rows // chunk
    lax.fori_loop(0, me * tiles, earlier, 0)

    state = state_s[...].astype(BF16)
    base = pl.multiple_of(me * rows, rows)
    for tile in range(tiles):
        key_features(pl.multiple_of(base + tile * chunk, chunk))
    for h in range(heads):
        lanes = slice(h * DH, (h + 1) * DH)
        for tile in range(tiles):
            r = slice(tile * chunk, (tile + 1) * chunk)
            q = q_ref[r, lanes]
            e = jnp.exp2(dot(jnp.concatenate([q, q], 1), wq_s[:, lanes]))
            sums = dot(e.astype(BF16), halves[:DH, :DH])
            qf_s[r, lanes] = (e / sums).astype(BF16)

    row_i = lax.broadcasted_iota(jnp.int32, (chunk, chunk), 0)
    col_i = lax.broadcasted_iota(jnp.int32, (chunk, chunk), 1)
    lower = col_i <= row_i
    upper = row_i <= col_i

    for tile in range(tiles):
        for c in range(tile + 1):
            teacher(
                pl.multiple_of(base + c * chunk, chunk), tile, chunk, lower if c == tile else None
            )

    def local(i):
        return pl.ds(pl.multiple_of(base + i * chunk, chunk), chunk)

    for h in range(heads):
        lanes = slice(h * DH, (h + 1) * DH)
        st = state[:, lanes]
        dkf = [None] * tiles
        dst = None
        gq = None
        for tile in range(tiles):
            r = slice(tile * chunk, (tile + 1) * chunk)
            qf = qf_s[r, lanes]
            nd = dot(qf, st, NT)
            for c in range(tile + 1):
                a = dot(qf, kf_s[local(c), lanes], NT)
                if c == tile:
                    a = jnp.where(lower, a, 0.0)
                nd += dot(a.astype(BF16), values_wide(base + c * chunk))
            inv = 1.0 / nd[:, DH:]
            student = nd[:, :DH] * inv
            out_ref[r, lanes] = student.astype(BF16)
            acc = acc_s[h, r, :]
            target = (acc[:, :DH] / acc[:, DH:]).astype(BF16).astype(F32)
            g = 2.0 * (student - target) * inv
            gden = -jnp.sum(g * student, -1, keepdims=True) * (1.0 / DH)
            ga = jnp.concatenate([g, jnp.broadcast_to(gden, g.shape)], 1).astype(BF16)
            dqf = dot(ga, st)
            for c in range(tile + 1):
                va = values_wide(base + c * chunk)
                da = dot(ga, va, NT)
                dat = dot(va, ga, NT)
                if c == tile:
                    da = jnp.where(lower, da, 0.0)
                    dat = jnp.where(upper, dat, 0.0)
                dqf += dot(da.astype(BF16), kf_s[local(c), lanes])
                piece = dot(dat.astype(BF16), qf)
                dkf[c] = piece if dkf[c] is None else dkf[c] + piece
            piece = dot(ga, qf, TN)
            dst = piece if dst is None else dst + piece
            u = qf.astype(F32) * dqf
            m = dot(u.astype(BF16), halves[:DH, :DH])
            dl = u - qf.astype(F32) * m
            piece = dot(q_ref[r, lanes], dl.astype(BF16), TN)
            gq = piece if gq is None else gq + piece
        gq_ref[h] = gq[:, :half] - gq[:, half:]
        dstate_s[:, lanes] = dst.astype(BF16)
        for c in range(tiles):
            f = kf_s[local(c), lanes].astype(F32)
            u = f * dkf[c]
            m = dot(u.astype(BF16), halves[:DH, :DH])
            dl = u - f * m
            gk_s[:, lanes] += dot(kv_ref[local(c), :DH], dl.astype(BF16), TN)

    def earlier_back(c, carry):
        first = pl.multiple_of(c * chunk, chunk)
        f = kf_s[pl.ds(first, chunk), :].astype(F32)
        u = f * dot(values_wide(first), dstate_s[...])
        dl = u - f * half_sums(u.astype(BF16))
        gk_s[...] += dot(kv_ref[pl.ds(first, chunk), :DH], dl.astype(BF16), TN)
        return carry

    lax.fori_loop(0, me * tiles, earlier_back, 0)
    for h in range(heads):
        gk_ref[h] = gk_s[:, h * DH : h * DH + half] - gk_s[:, h * DH + half : (h + 1) * DH]


def attention(chain_index, queries, kv, map_query, map_key, chunk=256):
    import functools

    rows, width = queries.shape
    heads = width // DH
    total = kv.shape[0]
    vmem = pl.BlockSpec(memory_space=pltpu.VMEM)
    return pl.pallas_call(
        functools.partial(attention_kernel, rows=rows, heads=heads, chunk=chunk),
        in_specs=[pl.BlockSpec(memory_space=pltpu.SMEM)] + [vmem] * 4,
        out_specs=[vmem] * 3,
        out_shape=[
            jax.ShapeDtypeStruct((rows, width), BF16),
            jax.ShapeDtypeStruct(map_query.shape, F32),
            jax.ShapeDtypeStruct(map_key.shape, F32),
        ],
        scratch_shapes=[
            pltpu.VMEM((2 * DH, width), BF16),
            pltpu.VMEM((2 * DH, width), BF16),
            pltpu.VMEM((total, width), BF16),
            pltpu.VMEM((rows, width), BF16),
            pltpu.VMEM((heads, rows, 2 * DH), F32),
            pltpu.VMEM((2 * DH, width), F32),
            pltpu.VMEM((2 * DH, width), BF16),
            pltpu.VMEM((DH, chunk), BF16),
            pltpu.VMEM((DH, width), F32),
        ],
        compiler_params=pltpu.CompilerParams(vmem_limit_bytes=56 * 2**20),
        name="attention",
    )(chain_index, queries, kv, map_query, map_key)


def per_device(tokens, w_query, w_key, w_value, map_query, map_key):
    row_count = tokens.shape[0]
    chain_index = lax.axis_index("seq")
    cosine, sine = rope_tables(row_count, DH, chain_index * row_count)
    own = jnp.concatenate([w_key, w_value], 1)
    other = partner(own, "head", 0)
    upper_half = lax.axis_index("head") % 2 == 1
    low = jnp.where(upper_half, other, own)
    high = jnp.where(upper_half, own, other)
    half = DH // 2
    w_kv = jnp.concatenate([low[:, :half], high[:, :half], low[:, half:], high[:, half:]], 1)
    gathered = lax.all_gather(tokens, "head", axis=0, tiled=False)
    queries, kv = project(gathered, w_query, w_kv, cosine, sine)
    kv = lax.all_gather(kv, "seq", axis=0, tiled=True)
    student_out, grad_query, grad_key = attention(
        jnp.full((1,), chain_index, jnp.int32), queries, kv, map_query, map_key
    )
    grads = jnp.stack([grad_query, grad_key])
    for apart in range(3):
        grads = grads + partner(grads, "seq", apart)
    return (student_out, grads[0], grads[1])


def solution(mesh):
    in_specs = (
        P("seq", "head"),
        P(None, "head"),
        P(None, "head"),
        P(None, "head"),
        P("head", None, None),
        P("head", None, None),
    )
    out_specs = (P("seq", "head"), P("head", None, None), P("head", None, None))
    return jax.shard_map(
        per_device, mesh=mesh, in_specs=in_specs, out_specs=out_specs, check_vma=False
    )
```

```python
import functools
import math

import jax
import jax.numpy as jnp
from jax import lax
from jax.experimental import pallas as pl
from jax.experimental.pallas import tpu as pltpu
from jax.sharding import PartitionSpec as P

DH = 128
ROPE_BASE = 500000.0
NT = (((1,), (1,)), ((), ()))
TN = (((0,), (0,)), ((), ()))
F32 = jnp.float32
BF16 = jnp.bfloat16


def partner(value, axis, apart):
    mask = 2**apart
    pairs = [(source, source ^ mask) for source in range(lax.axis_size(axis))]
    return lax.ppermute(value, axis, pairs)


def rope_tables(length, width, offset):
    half_width = width // 2
    positions = (offset + jnp.arange(length)).astype(F32)
    exponent = jnp.arange(half_width).astype(F32) * (2.0 / width)
    frequency = jnp.power(jnp.float32(ROPE_BASE), -exponent)
    angles = positions[:, None] * frequency[None, :]
    cosine, sine = jnp.cos(angles), jnp.sin(angles)
    return jnp.concatenate([cosine, cosine], 1), jnp.concatenate([-sine, sine], 1)


def dot(a, b, dims=None):
    if dims is None:
        return jnp.dot(a, b, preferred_element_type=F32)
    return lax.dot_general(a, b, dims, preferred_element_type=F32)


def gather_kernel(counts, begin, finish, *refs):
    table_ref = refs[0]
    n = len(counts)
    x_refs = refs[1 : 1 + n]
    wq_refs = refs[1 + n : 3 + n]
    wkv_refs = refs[3 + n : 5 + n]
    rest = refs[5 + n :]
    if begin:
        in_q, in_kv = rest[:2]
        rest = rest[2:]
    if finish:
        cos_ref, sin_ref, q_ref, kv_ref, acc_q, acc_kv = rest
    else:
        acc_q, acc_kv = rest
    step = pl.program_id(0)

    @pl.when(step == 0)
    def _():
        if begin:
            acc_q[...] = in_q[...]
            acc_kv[...] = in_kv[...]
        else:
            acc_q[...] = jnp.zeros_like(acc_q)
            acc_kv[...] = jnp.zeros_like(acc_kv)

    first = 0
    for x_ref, count in zip(x_refs, counts):

        @pl.when((step >= first) & (step < first + count))
        def _():
            acc_q[...] += dot(x_ref[0], wq_refs[0][...]) + dot(x_ref[1], wq_refs[1][...])
            acc_kv[...] += dot(x_ref[0], wkv_refs[0][...]) + dot(x_ref[1], wkv_refs[1][...])

        first += count

    if finish:

        @pl.when(step == pl.num_programs(0) - 1)
        def _():
            cosine = cos_ref[...]
            sine = sin_ref[...]
            for h in range(q_ref.shape[1] // DH):
                u = acc_q[:, h * DH : (h + 1) * DH]
                u = u * cosine + pltpu.roll(u, DH // 2, 1) * sine
                q_ref[:, h * DH : (h + 1) * DH] = u.astype(BF16)
            kv_ref[...] = acc_kv[...].astype(BF16)


def project(table, stacks, w_query, w_kv, start=None, tables=None):
    rows, depth = stacks[0].shape[1:]
    nq, nkv = w_query.shape[1], w_kv.shape[1]
    counts = [s.shape[0] // 2 for s in stacks]
    steps = sum(counts)
    in_specs = []
    first = 0
    for count in counts:
        in_specs.append(
            pl.BlockSpec(
                (2, rows, depth),
                lambda k, t, first=first, count=count: (jnp.clip(k - first, 0, count - 1), 0, 0),
            )
        )
        first += count
    for width in (nq, nkv):
        for j in range(2):
            in_specs.append(
                pl.BlockSpec((depth, width), lambda k, t, j=j: (t[2 * k + j], 0))
            )
    whole_q = pl.BlockSpec((rows, nq), lambda k, t: (0, 0))
    whole_kv = pl.BlockSpec((rows, nkv), lambda k, t: (0, 0))
    operands = [table, *stacks, w_query, w_query, w_kv, w_kv]
    if start is not None:
        in_specs += [whole_q, whole_kv]
        operands += list(start)
    scratch = []
    held = F32
    if tables is not None:
        in_specs += [pl.BlockSpec((rows, DH), lambda k, t: (0, 0))] * 2
        operands += list(tables)
        scratch = [pltpu.VMEM((rows, nq), F32), pltpu.VMEM((rows, nkv), F32)]
        held = BF16
    return pl.pallas_call(
        functools.partial(gather_kernel, counts, start is not None, tables is not None),
        grid_spec=pltpu.PrefetchScalarGridSpec(
            num_scalar_prefetch=1,
            grid=(steps,),
            in_specs=in_specs,
            out_specs=[whole_q, whole_kv],
            scratch_shapes=scratch,
        ),
        out_shape=[
            jax.ShapeDtypeStruct((rows, nq), held),
            jax.ShapeDtypeStruct((rows, nkv), held),
        ],
        compiler_params=pltpu.CompilerParams(vmem_limit_bytes=40 * 2**20),
        cost_estimate=pl.CostEstimate(
            flops=steps * 4 * rows * depth * (nq + nkv),
            bytes_accessed=steps * 4 * depth * (rows + nq + nkv),
            transcendentals=0,
        ),
        name="project",
    )(*operands)


def kv_kernel(upper_ref, own_ref, other_ref, cos_ref, sin_ref, kv_ref):
    half = DH // 2
    own = own_ref[...].astype(F32)
    other = other_ref[...].astype(F32)
    is_upper = upper_ref[0] == 1
    low = jnp.where(is_upper, other, own)
    high = jnp.where(is_upper, own, other)
    left = lax.broadcasted_iota(jnp.int32, low.shape, 1) < half
    keys = jnp.where(left, low, pltpu.roll(high, half, 1))
    values = jnp.where(left, pltpu.roll(low, half, 1), high)
    keys = keys * cos_ref[...] + pltpu.roll(keys, half, 1) * sin_ref[...]
    kv_ref[:, :DH] = keys.astype(BF16)
    kv_ref[:, DH:] = values.astype(BF16)


def join_kv(upper, own, other, cosine, sine):
    vmem = pl.BlockSpec(memory_space=pltpu.VMEM)
    return pl.pallas_call(
        kv_kernel,
        in_specs=[pl.BlockSpec(memory_space=pltpu.SMEM)] + [vmem] * 4,
        out_specs=vmem,
        out_shape=jax.ShapeDtypeStruct((own.shape[0], 2 * DH), BF16),
        name="join_kv",
    )(upper, own, other, cosine, sine)


def attention_kernel(
    chain_ref, q_ref, kv_ref, mq_ref, mk_ref,
    out_ref, gq_ref, gk_ref,
    wq_s, wk_s, kf_s, qf_s, acc_s, state_s, dstate_s, kt_s, gk_s,
    *, rows, heads, chunk,
):
    me = chain_ref[0]
    half = DH // 2
    fold = math.log2(math.e) / math.sqrt(DH)
    log2e = math.log2(math.e)

    i0 = lax.broadcasted_iota(jnp.int32, (2 * DH, 2 * DH), 0) // half
    i1 = lax.broadcasted_iota(jnp.int32, (2 * DH, 2 * DH), 1) // half
    halves = (i0 == i1).astype(F32).astype(BF16)

    def half_sums(u):
        width = u.shape[1]
        return jnp.concatenate(
            [dot(u[:, c : c + 2 * DH], halves) for c in range(0, width, 2 * DH)], 1
        )

    for h in range(heads):
        for src, dst in ((mq_ref, wq_s), (mk_ref, wk_s)):
            w = src[h] * log2e
            w = jnp.concatenate([w, -w], 1)
            high = w.astype(BF16)
            dst[:DH, h * DH : (h + 1) * DH] = high
            dst[DH:, h * DH : (h + 1) * DH] = (w - high.astype(F32)).astype(BF16)

    acc_s[...] = jnp.zeros_like(acc_s)
    state_s[...] = jnp.zeros_like(state_s)
    gk_s[...] = jnp.zeros_like(gk_s)
    ones = jnp.ones((chunk, DH), BF16)

    def key_features(first):
        k = kv_ref[pl.ds(first, chunk), :DH]
        e = jnp.exp2(dot(jnp.concatenate([k, k], 1), wk_s[...]))
        f = (e / half_sums(e.astype(BF16))).astype(BF16)
        kf_s[pl.ds(first, chunk), :] = f
        return f

    def values_wide(first):
        return jnp.concatenate([kv_ref[pl.ds(first, chunk), DH:], ones], 1)

    def teacher(first, tile, size, masked):
        k = kv_ref[pl.ds(first, chunk), :DH]
        va = values_wide(first)
        for h in range(heads):
            q = q_ref[tile * size : (tile + 1) * size, h * DH : (h + 1) * DH]
            p = jnp.exp2(dot(q, k, NT) * fold)
            if masked is not None:
                p = jnp.where(masked, p, 0.0)
            acc_s[h, tile * size : (tile + 1) * size, :] += dot(p.astype(BF16), va)

    def earlier(c, carry):
        first = pl.multiple_of(c * chunk, chunk)
        f = key_features(first)
        va = values_wide(first)
        state_s[...] += dot(va, f, TN)
        for tile in range(rows // chunk):
            teacher(first, tile, chunk, None)
        return carry

    tiles = rows // chunk
    begin = tiles * (2 - me % 2)
    end = tiles * 2 * (1 + me // 2)
    lax.fori_loop(begin, end, earlier, 0)

    state = state_s[...].astype(BF16)
    for tile in range(tiles):
        key_features(tile * chunk)
    for h in range(heads):
        lanes = slice(h * DH, (h + 1) * DH)
        for tile in range(tiles):
            r = slice(tile * chunk, (tile + 1) * chunk)
            q = q_ref[r, lanes]
            e = jnp.exp2(dot(jnp.concatenate([q, q], 1), wq_s[:, lanes]))
            sums = dot(e.astype(BF16), halves[:DH, :DH])
            qf_s[r, lanes] = (e / sums).astype(BF16)

    row_i = lax.broadcasted_iota(jnp.int32, (chunk, chunk), 0)
    col_i = lax.broadcasted_iota(jnp.int32, (chunk, chunk), 1)
    lower = col_i <= row_i
    upper = row_i <= col_i

    for tile in range(tiles):
        for c in range(tile + 1):
            teacher(
                c * chunk, tile, chunk, lower if c == tile else None
            )

    def local(i):
        return pl.ds(i * chunk, chunk)

    for h in range(heads):
        lanes = slice(h * DH, (h + 1) * DH)
        st = state[:, lanes]
        dkf = [None] * tiles
        dst = None
        gq = None
        for tile in range(tiles):
            r = slice(tile * chunk, (tile + 1) * chunk)
            qf = qf_s[r, lanes]
            nd = dot(qf, st, NT)
            for c in range(tile + 1):
                a = dot(qf, kf_s[local(c), lanes], NT)
                if c == tile:
                    a = jnp.where(lower, a, 0.0)
                nd += dot(a.astype(BF16), values_wide(c * chunk))
            inv = 1.0 / nd[:, DH:]
            student = nd[:, :DH] * inv
            out_ref[r, lanes] = student.astype(BF16)
            acc = acc_s[h, r, :]
            target = (acc[:, :DH] / acc[:, DH:]).astype(BF16).astype(F32)
            g = 2.0 * (student - target) * inv
            gden = -jnp.sum(g * student, -1, keepdims=True) * (1.0 / DH)
            ga = jnp.concatenate([g, jnp.broadcast_to(gden, g.shape)], 1).astype(BF16)
            dqf = dot(ga, st)
            for c in range(tile + 1):
                va = values_wide(c * chunk)
                da = dot(ga, va, NT)
                dat = dot(va, ga, NT)
                if c == tile:
                    da = jnp.where(lower, da, 0.0)
                    dat = jnp.where(upper, dat, 0.0)
                dqf += dot(da.astype(BF16), kf_s[local(c), lanes])
                piece = dot(dat.astype(BF16), qf)
                dkf[c] = piece if dkf[c] is None else dkf[c] + piece
            piece = dot(ga, qf, TN)
            dst = piece if dst is None else dst + piece
            u = qf.astype(F32) * dqf
            m = dot(u.astype(BF16), halves[:DH, :DH])
            dl = u - qf.astype(F32) * m
            piece = dot(q_ref[r, lanes], dl.astype(BF16), TN)
            gq = piece if gq is None else gq + piece
        gq_ref[h] = gq[:, :half] - gq[:, half:]
        dstate_s[:, lanes] = dst.astype(BF16)
        for c in range(tiles):
            f = kf_s[local(c), lanes].astype(F32)
            u = f * dkf[c]
            m = dot(u.astype(BF16), halves[:DH, :DH])
            dl = u - f * m
            gk_s[:, lanes] += dot(kv_ref[local(c), :DH], dl.astype(BF16), TN)

    def earlier_back(c, carry):
        first = pl.multiple_of(c * chunk, chunk)
        f = kf_s[pl.ds(first, chunk), :].astype(F32)
        u = f * dot(values_wide(first), dstate_s[...])
        dl = u - f * half_sums(u.astype(BF16))
        gk_s[...] += dot(kv_ref[pl.ds(first, chunk), :DH], dl.astype(BF16), TN)
        return carry

    lax.fori_loop(begin, end, earlier_back, 0)
    for h in range(heads):
        gk_ref[h] = gk_s[:, h * DH : h * DH + half] - gk_s[:, h * DH + half : (h + 1) * DH]


def attention(chain_index, queries, kv, map_query, map_key, chunk=256):
    rows, width = queries.shape
    heads = width // DH
    total = kv.shape[0]
    vmem = pl.BlockSpec(memory_space=pltpu.VMEM)
    return pl.pallas_call(
        functools.partial(attention_kernel, rows=rows, heads=heads, chunk=chunk),
        in_specs=[pl.BlockSpec(memory_space=pltpu.SMEM)] + [vmem] * 4,
        out_specs=[vmem] * 3,
        out_shape=[
            jax.ShapeDtypeStruct((rows, width), BF16),
            jax.ShapeDtypeStruct(map_query.shape, F32),
            jax.ShapeDtypeStruct(map_key.shape, F32),
        ],
        scratch_shapes=[
            pltpu.VMEM((2 * DH, width), BF16),
            pltpu.VMEM((2 * DH, width), BF16),
            pltpu.VMEM((total, width), BF16),
            pltpu.VMEM((rows, width), BF16),
            pltpu.VMEM((heads, rows, 2 * DH), F32),
            pltpu.VMEM((2 * DH, width), F32),
            pltpu.VMEM((2 * DH, width), BF16),
            pltpu.VMEM((DH, chunk), BF16),
            pltpu.VMEM((DH, width), F32),
        ],
        compiler_params=pltpu.CompilerParams(vmem_limit_bytes=56 * 2**20),
        name="attention",
    )(chain_index, queries, kv, map_query, map_key)


def hop_x(value, by):
    pairs = [(4 * z + x, 4 * z + (x + by) % 4) for z in range(4) for x in range(4)]
    return lax.ppermute(value, "head", pairs)


def hop_z(value, by):
    pairs = [(4 * z + x, 4 * ((z + by) % 4) + x) for z in range(4) for x in range(4)]
    return lax.ppermute(value, "head", pairs)


def hop_y(value, pairs):
    return lax.ppermute(
        value, "seq", [(2 * a + core, 2 * b + core) for a, b in pairs for core in range(2)]
    )


def ring(stack, hop):
    left = hop(stack, 1)
    right = hop(stack, -1)
    return left, right


def per_device(tokens, w_query, w_key, w_value, map_query, map_key):
    row_count, depth = tokens.shape
    half = depth // 2
    chain_index = lax.axis_index("seq")
    place = lax.axis_index("head")
    z, x = place // 4, place % 4
    order = (0, 3, 1, 2)
    xs = [(x + d) % 4 for d in order]
    zs = [(z + d) % 4 for d in order]

    first, second = tokens[:, :half], tokens[:, half:]
    a = [first, hop_x(first, 1), hop_x(first, -1), hop_x(first, 2)]
    b = [second, hop_z(second, 1), hop_z(second, -1), hop_z(second, 2)]
    stack_a = jnp.stack(a)
    stack_b = jnp.stack(b)
    a_left, a_right = ring(stack_a, hop_z)
    b_left, b_right = ring(stack_b, hop_x)
    a_far0 = hop_z(a_left[:2], 1)
    a_far1 = hop_z(a_right[2:], -1)
    b_far0 = hop_x(b_left[:2], 1)
    b_far1 = hop_x(b_right[2:], -1)

    def at_a(zz, which):
        return [2 * (4 * zz + xs[k]) for k in which]

    def at_b(xx, which):
        return [2 * (4 * zs[k] + xx) + 1 for k in which]

    def table(*parts):
        return jnp.stack([v for p in parts for v in p]).astype(jnp.int32)

    every = range(4)
    w_kv = jnp.concatenate([w_key, w_value], 1)
    cosine, sine = rope_tables(row_count, DH, chain_index * row_count)
    acc = project(
        table(at_a(z, every), at_b(x, every)), [stack_a, stack_b], w_query, w_kv
    )
    acc = project(
        table(at_a(zs[1], every), at_a(zs[2], every), at_b(xs[1], every), at_b(xs[2], every)),
        [a_left, a_right, b_left, b_right], w_query, w_kv, acc,
    )
    queries, own = project(
        table(at_a(zs[3], (0, 1)), at_a(zs[3], (2, 3)), at_b(xs[3], (0, 1)), at_b(xs[3], (2, 3))),
        [a_far0, a_far1, b_far0, b_far1], w_query, w_kv, acc, (cosine, sine),
    )
    other = partner(own, "head", 0)
    upper = jnp.full((1,), place % 2, jnp.int32)
    kv = join_kv(upper, own, other, cosine, sine)

    below = hop_y(kv, [(0, 1), (1, 2), (2, 3)])
    below3 = hop_y(kv, [(0, 3)])
    below2 = hop_y(kv, [(0, 2), (1, 3)])
    mate = partner(kv, "seq", 0)
    stack = jnp.stack([below, below2, below3])
    stack_mate = partner(stack, "seq", 0)
    blocks = jnp.concatenate(
        [kv, mate, stack[0], stack_mate[0], stack[1], stack_mate[1], stack[2], stack_mate[2]], 0
    )
    student_out, grad_query, grad_key = attention(
        jnp.full((1,), chain_index, jnp.int32), queries, blocks, map_query, map_key
    )
    grads = jnp.stack([grad_query, grad_key])
    for apart in range(3):
        grads = grads + partner(grads, "seq", apart)
    return (student_out, grads[0], grads[1])


def solution(mesh):
    in_specs = (
        P("seq", "head"),
        P(None, "head"),
        P(None, "head"),
        P(None, "head"),
        P("head", None, None),
        P("head", None, None),
    )
    out_specs = (P("seq", "head"), P("head", None, None), P("head", None, None))
    return jax.shard_map(
        per_device, mesh=mesh, in_specs=in_specs, out_specs=out_specs, check_vma=False
    )
```

```python
import functools
import math

import jax
import jax.numpy as jnp
from jax import lax
from jax.experimental import pallas as pl
from jax.experimental.pallas import tpu as pltpu
from jax.sharding import PartitionSpec as P

DH = 128
ROPE_BASE = 500000.0
NT = (((1,), (1,)), ((), ()))
TN = (((0,), (0,)), ((), ()))
F32 = jnp.float32
BF16 = jnp.bfloat16


def partner(value, axis, apart):
    mask = 2**apart
    pairs = [(source, source ^ mask) for source in range(lax.axis_size(axis))]
    return lax.ppermute(value, axis, pairs)


def rope_tables(length, width, offset):
    half_width = width // 2
    positions = (offset + jnp.arange(length)).astype(F32)
    exponent = jnp.arange(half_width).astype(F32) * (2.0 / width)
    frequency = jnp.power(jnp.float32(ROPE_BASE), -exponent)
    angles = positions[:, None] * frequency[None, :]
    cosine, sine = jnp.cos(angles), jnp.sin(angles)
    return jnp.concatenate([cosine, cosine], 1), jnp.concatenate([-sine, sine], 1)


def dot(a, b, dims=None):
    if dims is None:
        return jnp.dot(a, b, preferred_element_type=F32)
    return lax.dot_general(a, b, dims, preferred_element_type=F32)


def gather_kernel(counts, begin, finish, *refs):
    table_ref = refs[0]
    n = len(counts)
    x_refs = refs[1 : 1 + n]
    wq_refs = refs[1 + n : 3 + n]
    wkv_refs = refs[3 + n : 5 + n]
    rest = refs[5 + n :]
    if begin:
        in_q, in_kv = rest[:2]
        rest = rest[2:]
    if finish:
        cos_ref, sin_ref, q_ref, kv_ref, acc_q, acc_kv = rest
    else:
        acc_q, acc_kv = rest
    step = pl.program_id(0)

    @pl.when(step == 0)
    def _():
        if begin:
            acc_q[...] = in_q[...]
            acc_kv[...] = in_kv[...]
        else:
            acc_q[...] = jnp.zeros_like(acc_q)
            acc_kv[...] = jnp.zeros_like(acc_kv)

    first = 0
    for x_ref, count in zip(x_refs, counts):

        @pl.when((step >= first) & (step < first + count))
        def _():
            acc_q[...] += dot(x_ref[0], wq_refs[0][...]) + dot(x_ref[1], wq_refs[1][...])
            acc_kv[...] += dot(x_ref[0], wkv_refs[0][...]) + dot(x_ref[1], wkv_refs[1][...])

        first += count

    if finish:

        @pl.when(step == pl.num_programs(0) - 1)
        def _():
            cosine = cos_ref[...]
            sine = sin_ref[...]
            for h in range(q_ref.shape[1] // DH):
                u = acc_q[:, h * DH : (h + 1) * DH]
                u = u * cosine + pltpu.roll(u, DH // 2, 1) * sine
                q_ref[:, h * DH : (h + 1) * DH] = u.astype(BF16)
            kv_ref[...] = acc_kv[...].astype(BF16)


def project(table, stacks, w_query, w_kv, start=None, tables=None):
    rows, depth = stacks[0].shape[1:]
    nq, nkv = w_query.shape[1], w_kv.shape[1]
    counts = [s.shape[0] // 2 for s in stacks]
    steps = sum(counts)
    in_specs = []
    first = 0
    for count in counts:
        in_specs.append(
            pl.BlockSpec(
                (2, rows, depth),
                lambda k, t, first=first, count=count: (jnp.clip(k - first, 0, count - 1), 0, 0),
            )
        )
        first += count
    for width in (nq, nkv):
        for j in range(2):
            in_specs.append(
                pl.BlockSpec((depth, width), lambda k, t, j=j: (t[2 * k + j], 0))
            )
    whole_q = pl.BlockSpec((rows, nq), lambda k, t: (0, 0))
    whole_kv = pl.BlockSpec((rows, nkv), lambda k, t: (0, 0))
    operands = [table, *stacks, w_query, w_query, w_kv, w_kv]
    if start is not None:
        in_specs += [whole_q, whole_kv]
        operands += list(start)
    scratch = []
    held = F32
    if tables is not None:
        in_specs += [pl.BlockSpec((rows, DH), lambda k, t: (0, 0))] * 2
        operands += list(tables)
        scratch = [pltpu.VMEM((rows, nq), F32), pltpu.VMEM((rows, nkv), F32)]
        held = BF16
    return pl.pallas_call(
        functools.partial(gather_kernel, counts, start is not None, tables is not None),
        grid_spec=pltpu.PrefetchScalarGridSpec(
            num_scalar_prefetch=1,
            grid=(steps,),
            in_specs=in_specs,
            out_specs=[whole_q, whole_kv],
            scratch_shapes=scratch,
        ),
        out_shape=[
            jax.ShapeDtypeStruct((rows, nq), held),
            jax.ShapeDtypeStruct((rows, nkv), held),
        ],
        compiler_params=pltpu.CompilerParams(vmem_limit_bytes=40 * 2**20),
        cost_estimate=pl.CostEstimate(
            flops=steps * 4 * rows * depth * (nq + nkv),
            bytes_accessed=steps * 4 * depth * (rows + nq + nkv),
            transcendentals=0,
        ),
        name="project",
    )(*operands)


def kv_kernel(upper_ref, own_ref, other_ref, cos_ref, sin_ref, kv_ref):
    half = DH // 2
    own = own_ref[...].astype(F32)
    other = other_ref[...].astype(F32)
    is_upper = upper_ref[0] == 1
    low = jnp.where(is_upper, other, own)
    high = jnp.where(is_upper, own, other)
    left = lax.broadcasted_iota(jnp.int32, low.shape, 1) < half
    keys = jnp.where(left, low, pltpu.roll(high, half, 1))
    values = jnp.where(left, pltpu.roll(low, half, 1), high)
    keys = keys * cos_ref[...] + pltpu.roll(keys, half, 1) * sin_ref[...]
    kv_ref[:, :DH] = keys.astype(BF16)
    kv_ref[:, DH:] = values.astype(BF16)


def join_kv(upper, own, other, cosine, sine):
    vmem = pl.BlockSpec(memory_space=pltpu.VMEM)
    return pl.pallas_call(
        kv_kernel,
        in_specs=[pl.BlockSpec(memory_space=pltpu.SMEM)] + [vmem] * 4,
        out_specs=vmem,
        out_shape=jax.ShapeDtypeStruct((own.shape[0], 2 * DH), BF16),
        name="join_kv",
    )(upper, own, other, cosine, sine)


def half_ones():
    half = DH // 2
    i0 = lax.broadcasted_iota(jnp.int32, (2 * DH, 2 * DH), 0) // half
    i1 = lax.broadcasted_iota(jnp.int32, (2 * DH, 2 * DH), 1) // half
    return (i0 == i1).astype(F32).astype(BF16)


def half_sums(u, halves):
    return jnp.concatenate(
        [dot(u[:, c : c + 2 * DH], halves) for c in range(0, u.shape[1], 2 * DH)], 1
    )


def wide_map(m_ref, heads):
    highs, lows = [], []
    for h in range(heads):
        w = m_ref[h] * math.log2(math.e)
        w = jnp.concatenate([w, -w], 1)
        high = w.astype(BF16)
        highs.append(high)
        lows.append((w - high.astype(F32)).astype(BF16))
    return jnp.concatenate([jnp.concatenate(highs, 1), jnp.concatenate(lows, 1)], 0)


def features(rows, w, halves):
    e = jnp.exp2(dot(jnp.concatenate([rows, rows], 1), w))
    return (e / half_sums(e.astype(BF16), halves)).astype(BF16)


def query_kernel(q_ref, m_ref, qf_ref):
    halves = half_ones()
    heads = m_ref.shape[0]
    w = wide_map(m_ref, heads)
    for h in range(0, heads, 2):
        for r in range(0, q_ref.shape[0], 256):
            parts = []
            for g in (h, h + 1):
                q = q_ref[r : r + 256, g * DH : (g + 1) * DH]
                logits = dot(jnp.concatenate([q, q], 1), w[:, g * DH : (g + 1) * DH])
                parts.append(jnp.exp2(logits))
            e = jnp.concatenate(parts, 1)
            f = e / dot(e.astype(BF16), halves)
            qf_ref[r : r + 256, h * DH : (h + 2) * DH] = f.astype(BF16)


def query_features(queries, map_query):
    vmem = pl.BlockSpec(memory_space=pltpu.VMEM)
    rows, width = queries.shape
    return pl.pallas_call(
        query_kernel,
        in_specs=[vmem] * 2,
        out_specs=vmem,
        out_shape=jax.ShapeDtypeStruct((rows, width), BF16),
        compiler_params=pltpu.CompilerParams(vmem_limit_bytes=24 * 2**20),
        cost_estimate=pl.CostEstimate(
            flops=rows * width * 1024, bytes_accessed=4 * rows * width, transcendentals=rows * width
        ),
        name="query_features",
    )(queries, map_query)


FOLD = math.log2(math.e) / math.sqrt(DH)


def local_kernel(q_ref, qf_ref, kv_ref, mk_ref, kf_ref, acc_ref, nd_ref, *, tile):
    halves = half_ones()
    rows = q_ref.shape[0]
    heads = mk_ref.shape[0]
    w = wide_map(mk_ref, heads)
    tiles = rows // tile
    for i in range(tiles):
        r = slice(i * tile, (i + 1) * tile)
        kf_ref[r, :] = features(kv_ref[r, :DH], w, halves)
    row_i = lax.broadcasted_iota(jnp.int32, (tile, tile), 0)
    col_i = lax.broadcasted_iota(jnp.int32, (tile, tile), 1)
    lower = col_i <= row_i
    ones = jnp.ones((rows, DH), BF16)
    for i in range(tiles):
        r = slice(i * tile, (i + 1) * tile)
        n = (i + 1) * tile
        va = jnp.concatenate([kv_ref[:n, DH:], ones[:n]], 1)
        for h in range(heads):
            lanes = slice(h * DH, (h + 1) * DH)

            def masked(u):
                last = jnp.where(lower, u[:, n - tile :], 0.0)
                return last if i == 0 else jnp.concatenate([u[:, : n - tile], last], 1)

            p = masked(jnp.exp2(dot(q_ref[r, lanes], kv_ref[:n, :DH], NT) * FOLD))
            acc_ref[h, r, :] = dot(p.astype(BF16), va)
            a = masked(dot(qf_ref[r, lanes], kf_ref[:n, lanes], NT))
            nd_ref[h, r, :] = dot(a.astype(BF16), va)


def local_part(queries, query_feats, kv, map_key, tile=256):
    rows, width = queries.shape
    heads = width // DH
    vmem = pl.BlockSpec(memory_space=pltpu.VMEM)
    wide = jax.ShapeDtypeStruct((heads, rows, 2 * DH), F32)
    return pl.pallas_call(
        functools.partial(local_kernel, tile=tile),
        in_specs=[vmem] * 4,
        out_specs=[vmem] * 3,
        out_shape=[jax.ShapeDtypeStruct((rows, width), BF16), wide, wide],
        compiler_params=pltpu.CompilerParams(vmem_limit_bytes=32 * 2**20),
        cost_estimate=pl.CostEstimate(
            flops=6 * rows * rows * width,
            bytes_accessed=20 * rows * width,
            transcendentals=rows * rows * heads,
        ),
        name="local_part",
    )(queries, query_feats, kv, map_key)


def attention_kernel(
    chain_ref, q_ref, qf_ref, kf_ref, acc_in, nd_in, kv_ref, mate_ref, stack_ref, smate_ref, mk_ref,
    out_ref, g_ref,
    kv_s, kf_s, acc_s, state_s, dstate_s, gk_s,
    *, tile,
):
    core = chain_ref[0] % 2
    chips = chain_ref[0] // 2
    rows = q_ref.shape[0]
    heads = mk_ref.shape[0]
    tiles = rows // tile
    half = DH // 2
    halves = half_ones()
    pair = halves[:DH, :DH]
    w_key = wide_map(mk_ref, heads)

    far = stack_ref.shape[0]
    kv_s[:rows, :] = mate_ref[...]
    kv_s[rows : rows + far, :] = stack_ref[...]
    kv_s[rows + far :, :] = smate_ref[...]
    acc_s[...] = jnp.zeros_like(acc_s)
    state_s[...] = jnp.zeros_like(state_s)
    gk_s[...] = jnp.zeros_like(gk_s)
    ones = jnp.ones((rows, DH), BF16)

    def block_first(j):
        place = jnp.where(j < chips, 1 + j, 4 + j - chips)
        place = jnp.where(j < 2 * chips, place, 0)
        return place * rows

    def earlier(j, carry):
        first = block_first(j)
        for i in range(tiles):
            at = pl.multiple_of(first + i * tile, tile)
            f = features(kv_s[pl.ds(at, tile), :DH], w_key, halves)
            kf_s[pl.ds(at, tile), :] = f
            va = jnp.concatenate([kv_s[pl.ds(at, tile), DH:], ones[:tile]], 1)
            state_s[...] += dot(va, f, TN)
        at = pl.multiple_of(first, rows)
        k = kv_s[pl.ds(at, rows), :DH]
        va = jnp.concatenate([kv_s[pl.ds(at, rows), DH:], ones], 1)
        for h in range(heads):
            for i in range(tiles):
                r = slice(i * tile, (i + 1) * tile)
                p = jnp.exp2(dot(q_ref[r, h * DH : (h + 1) * DH], k, NT) * FOLD)
                acc_s[h, r, :] += dot(p.astype(BF16), va)
        return carry

    blocks = 2 * chips + core
    lax.fori_loop(0, blocks, earlier, 0)

    state = state_s[...].astype(BF16)
    row_i = lax.broadcasted_iota(jnp.int32, (tile, tile), 0)
    col_i = lax.broadcasted_iota(jnp.int32, (tile, tile), 1)
    lower = col_i <= row_i
    upper = row_i <= col_i

    def span(i):
        return slice(i * tile, (i + 1) * tile)

    def own_values(i):
        return jnp.concatenate([kv_ref[span(i), DH:], ones[:tile]], 1)

    for h in range(heads):
        lanes = slice(h * DH, (h + 1) * DH)
        st = state[:, lanes]
        dkf = [None] * tiles
        dst = None
        gq = None
        for i in range(tiles):
            r = span(i)
            qf = qf_ref[r, lanes]
            nd = nd_in[h, r, :] + dot(qf, st, NT)
            inv = 1.0 / nd[:, DH:]
            student = nd[:, :DH] * inv
            out_ref[r, lanes] = student.astype(BF16)
            acc = acc_in[h, r, :] + acc_s[h, r, :]
            target = (acc[:, :DH] / acc[:, DH:]).astype(BF16).astype(F32)
            g = 2.0 * (student - target) * inv
            gden = -jnp.sum(g * student, -1, keepdims=True) * (1.0 / DH)
            ga = jnp.concatenate([g, jnp.broadcast_to(gden, g.shape)], 1).astype(BF16)
            dqf = dot(ga, st)
            for c in range(i + 1):
                va = own_values(c)
                da = dot(ga, va, NT)
                dat = dot(va, ga, NT)
                if c == i:
                    da = jnp.where(lower, da, 0.0)
                    dat = jnp.where(upper, dat, 0.0)
                dqf += dot(da.astype(BF16), kf_ref[span(c), lanes])
                piece = dot(dat.astype(BF16), qf)
                dkf[c] = piece if dkf[c] is None else dkf[c] + piece
            piece = dot(ga, qf, TN)
            dst = piece if dst is None else dst + piece
            u = qf.astype(F32) * dqf
            dl = u - qf.astype(F32) * dot(u.astype(BF16), pair)
            piece = dot(q_ref[r, lanes], dl.astype(BF16), TN)
            gq = piece if gq is None else gq + piece
        g_ref[h, :, :half] = gq[:, :half] - gq[:, half:]
        dstate_s[:, lanes] = dst.astype(BF16)
        for c in range(tiles):
            f = kf_ref[span(c), lanes].astype(F32)
            u = f * dkf[c]
            dl = u - f * dot(u.astype(BF16), pair)
            gk_s[:, lanes] += dot(kv_ref[span(c), :DH], dl.astype(BF16), TN)

    def earlier_back(j, carry):
        first = block_first(j)
        for i in range(tiles):
            at = pl.multiple_of(first + i * tile, tile)
            va = jnp.concatenate([kv_s[pl.ds(at, tile), DH:], ones[:tile]], 1)
            f = kf_s[pl.ds(at, tile), :].astype(F32)
            u = f * dot(va, dstate_s[...])
            dl = u - f * half_sums(u.astype(BF16), halves)
            gk_s[...] += dot(kv_s[pl.ds(at, tile), :DH], dl.astype(BF16), TN)
        return carry

    lax.fori_loop(0, blocks, earlier_back, 0)
    for h in range(heads):
        left = gk_s[:, h * DH : h * DH + half]
        g_ref[h, :, half:] = left - gk_s[:, h * DH + half : (h + 1) * DH]


def attention(chain_index, queries, query_feats, local, kv, mate, stack, stack_mate, map_key, tile=256):
    rows, width = queries.shape
    heads = width // DH
    earlier = rows + 2 * stack.shape[0]
    vmem = pl.BlockSpec(memory_space=pltpu.VMEM)
    return pl.pallas_call(
        functools.partial(attention_kernel, tile=tile),
        in_specs=[pl.BlockSpec(memory_space=pltpu.SMEM)] + [vmem] * 10,
        out_specs=[vmem] * 2,
        out_shape=[
            jax.ShapeDtypeStruct((rows, width), BF16),
            jax.ShapeDtypeStruct((heads, DH, DH), F32),
        ],
        scratch_shapes=[
            pltpu.VMEM((earlier, 2 * DH), BF16),
            pltpu.VMEM((earlier, width), BF16),
            pltpu.VMEM((heads, rows, 2 * DH), F32),
            pltpu.VMEM((2 * DH, width), F32),
            pltpu.VMEM((2 * DH, width), BF16),
            pltpu.VMEM((DH, width), F32),
        ],
        compiler_params=pltpu.CompilerParams(vmem_limit_bytes=56 * 2**20),
        name="attention",
    )(chain_index, queries, query_feats, *local, kv, mate, stack, stack_mate, map_key)


def hop_x(value, by):
    pairs = [(4 * z + x, 4 * z + (x + by) % 4) for z in range(4) for x in range(4)]
    return lax.ppermute(value, "head", pairs)


def hop_z(value, by):
    pairs = [(4 * z + x, 4 * ((z + by) % 4) + x) for z in range(4) for x in range(4)]
    return lax.ppermute(value, "head", pairs)


def hop_y(value, pairs):
    return lax.ppermute(
        value, "seq", [(2 * a + core, 2 * b + core) for a, b in pairs for core in range(2)]
    )


def per_device(tokens, w_query, w_key, w_value, map_query, map_key):
    row_count, depth = tokens.shape
    half = depth // 2
    chain_index = lax.axis_index("seq")
    place = lax.axis_index("head")
    z, x = place // 4, place % 4
    order = (0, 3, 1, 2)
    xs = [(x + d) % 4 for d in order]
    zs = [(z + d) % 4 for d in order]

    first, second = tokens[:, :half], tokens[:, half:]
    a = [first, hop_x(first, 1), hop_x(first, -1), hop_x(first, 2)]
    b = [second, hop_z(second, 1), hop_z(second, -1), hop_z(second, 2)]
    a0, a1 = jnp.stack(a[:2]), jnp.stack(a[2:])
    b0, b1 = jnp.stack(b[:2]), jnp.stack(b[2:])
    a0_left, a0_right = hop_z(a0, 1), hop_z(a0, -1)
    b0_left, b0_right = hop_x(b0, 1), hop_x(b0, -1)
    a1_left, a1_right = hop_z(a1, 1), hop_z(a1, -1)
    b1_left, b1_right = hop_x(b1, 1), hop_x(b1, -1)

    def at_a(zz, which):
        return [2 * (4 * zz + xs[k]) for k in which]

    def at_b(xx, which):
        return [2 * (4 * zs[k] + xx) + 1 for k in which]

    def table(*parts):
        return jnp.stack([v for p in parts for v in p]).astype(jnp.int32)

    every = range(4)
    w_kv = jnp.concatenate([w_key, w_value], 1)
    cosine, sine = rope_tables(row_count, DH, chain_index * row_count)
    near, away = (0, 1), (2, 3)
    acc = project(
        table(at_a(z, every), at_b(x, every)), [a0, a1, b0, b1], w_query, w_kv
    )
    acc, a0_left, a1_right, b0_left, b1_right = lax.optimization_barrier(
        (acc, a0_left, a1_right, b0_left, b1_right)
    )
    a0_far, a1_far = hop_z(a0_left, 1), hop_z(a1_right, -1)
    b0_far, b1_far = hop_x(b0_left, 1), hop_x(b1_right, -1)
    acc = project(
        table(
            at_a(zs[1], every), at_a(zs[2], every), at_b(xs[1], every), at_b(xs[2], every)
        ),
        [a0_left, a1_left, a0_right, a1_right, b0_left, b1_left, b0_right, b1_right],
        w_query, w_kv, acc,
    )
    queries, own = project(
        table(at_a(zs[3], near), at_a(zs[3], away), at_b(xs[3], near), at_b(xs[3], away)),
        [a0_far, a1_far, b0_far, b1_far], w_query, w_kv, acc, (cosine, sine),
    )
    other = partner(own, "head", 0)
    query_feats = query_features(queries, map_query)
    upper = jnp.full((1,), place % 2, jnp.int32)
    kv = join_kv(upper, own, other, cosine, sine)

    below = hop_y(kv, [(0, 1), (1, 2), (2, 3)])
    below3 = hop_y(kv, [(0, 3)])
    below2 = hop_y(kv, [(0, 2), (1, 3)])
    mate = partner(kv, "seq", 0)
    local = local_part(queries, query_feats, kv, map_key)
    stack = jnp.concatenate([below, below2, below3], 0)
    stack_mate = partner(stack, "seq", 0)
    student_out, grads = attention(
        jnp.full((1,), chain_index, jnp.int32),
        queries, query_feats, local, kv, mate, stack, stack_mate, map_key,
    )

    core = chain_index % 2
    mine = grads.shape[0] // 2
    kept = lax.dynamic_slice_in_dim(grads, core * mine, mine, 0)
    given = lax.dynamic_slice_in_dim(grads, (1 - core) * mine, mine, 0)
    kept = kept + partner(given, "seq", 0)
    ahead = hop_y(kept, [(y, (y + 1) % 4) for y in range(4)])
    behind = hop_y(kept, [(y, (y + 3) % 4) for y in range(4)])
    across = hop_y(kept, [(y, (y + 2) % 4) for y in range(4)])
    kept = (kept + across) + (ahead + behind)
    given = partner(kept, "seq", 0)
    grads = jnp.where(
        core == 0, jnp.concatenate([kept, given], 0), jnp.concatenate([given, kept], 0)
    )
    half = DH // 2
    return (student_out, grads[:, :, :half], grads[:, :, half:])


def solution(mesh):
    in_specs = (
        P("seq", "head"),
        P(None, "head"),
        P(None, "head"),
        P(None, "head"),
        P("head", None, None),
        P("head", None, None),
    )
    out_specs = (P("seq", "head"), P("head", None, None), P("head", None, None))
    return jax.shard_map(
        per_device, mesh=mesh, in_specs=in_specs, out_specs=out_specs, check_vma=False
    )
```

```python
import functools
import math

import jax
import jax.numpy as jnp
from jax import lax
from jax.experimental import pallas as pl
from jax.experimental.pallas import tpu as pltpu
from jax.sharding import PartitionSpec as P

DH = 128
ROPE_BASE = 500000.0
NT = (((1,), (1,)), ((), ()))
TN = (((0,), (0,)), ((), ()))
F32 = jnp.float32
BF16 = jnp.bfloat16


def partner(value, axis, apart):
    mask = 2**apart
    pairs = [(source, source ^ mask) for source in range(lax.axis_size(axis))]
    return lax.ppermute(value, axis, pairs)


def rope_tables(length, width, offset):
    half_width = width // 2
    positions = (offset + jnp.arange(length)).astype(F32)
    exponent = jnp.arange(half_width).astype(F32) * (2.0 / width)
    frequency = jnp.power(jnp.float32(ROPE_BASE), -exponent)
    angles = positions[:, None] * frequency[None, :]
    cosine, sine = jnp.cos(angles), jnp.sin(angles)
    return jnp.concatenate([cosine, cosine], 1), jnp.concatenate([-sine, sine], 1)


def dot(a, b, dims=None):
    if dims is None:
        return jnp.dot(a, b, preferred_element_type=F32)
    return lax.dot_general(a, b, dims, preferred_element_type=F32)


def gather_kernel(counts, widths, begin, turned, *refs):
    table_ref = refs[0]
    n, m = len(counts), len(widths)
    x_refs = refs[1 : 1 + n]
    w_refs = refs[1 + n : 1 + n + 2 * m]
    rest = refs[1 + n + 2 * m :]
    if begin:
        ins = rest[:m]
        rest = rest[m:]
    if turned is not None:
        if turned:
            cos_ref, sin_ref = rest[:2]
            rest = rest[2:]
        outs, accs = rest[:m], rest[m:]
    else:
        accs = rest
    step = pl.program_id(0)

    @pl.when(step == 0)
    def _():
        for k in range(m):
            accs[k][...] = ins[k][...] if begin else jnp.zeros_like(accs[k])

    first = 0
    for x_ref, count in zip(x_refs, counts):

        @pl.when((step >= first) & (step < first + count))
        def _():
            for k in range(m):
                accs[k][...] += dot(x_ref[0], w_refs[2 * k][...]) + dot(
                    x_ref[1], w_refs[2 * k + 1][...]
                )

        first += count

    if turned is not None:

        @pl.when(step == pl.num_programs(0) - 1)
        def _():
            for out, acc in zip(outs, accs):
                if turned:
                    for h in range(out.shape[1] // DH):
                        u = acc[:, h * DH : (h + 1) * DH]
                        u = u * cos_ref[...] + pltpu.roll(u, DH // 2, 1) * sin_ref[...]
                        out[:, h * DH : (h + 1) * DH] = u.astype(BF16)
                else:
                    out[...] = acc[...].astype(BF16)


def project(table, stacks, weights, start=None, final=None):
    rows, depth = stacks[0].shape[1:]
    widths = [w.shape[1] for w in weights]
    counts = [s.shape[0] // 2 for s in stacks]
    steps = sum(counts)
    in_specs = []
    first = 0
    for count in counts:
        in_specs.append(
            pl.BlockSpec(
                (2, rows, depth),
                lambda k, t, first=first, count=count: (jnp.clip(k - first, 0, count - 1), 0, 0),
            )
        )
        first += count
    operands = [table, *stacks]
    for w in weights:
        for j in range(2):
            in_specs.append(
                pl.BlockSpec((depth, w.shape[1]), lambda k, t, j=j: (t[2 * k + j], 0))
            )
            operands.append(w)
    whole = [pl.BlockSpec((rows, width), lambda k, t: (0, 0)) for width in widths]
    if start is not None:
        in_specs += whole
        operands += list(start)
    scratch = []
    held = F32
    if final is not None:
        in_specs += [pl.BlockSpec((rows, DH), lambda k, t: (0, 0))] * len(final)
        operands += list(final)
        scratch = [pltpu.VMEM((rows, width), F32) for width in widths]
        held = BF16
    return pl.pallas_call(
        functools.partial(
            gather_kernel, counts, widths, start is not None, None if final is None else bool(final)
        ),
        grid_spec=pltpu.PrefetchScalarGridSpec(
            num_scalar_prefetch=1,
            grid=(steps,),
            in_specs=in_specs,
            out_specs=whole,
            scratch_shapes=scratch,
        ),
        out_shape=[jax.ShapeDtypeStruct((rows, width), held) for width in widths],
        compiler_params=pltpu.CompilerParams(vmem_limit_bytes=40 * 2**20),
        cost_estimate=pl.CostEstimate(
            flops=steps * 4 * rows * depth * sum(widths),
            bytes_accessed=steps * 4 * depth * (rows + sum(widths)),
            transcendentals=0,
        ),
        name="project",
    )(*operands)


def split_kernel(*refs):
    n = len(refs) // 2
    for k in range(n):
        refs[n + k][...] = refs[k][...]


def halves_of(stacks, ends):
    rows, depth = stacks[0].shape[1:]
    return pl.pallas_call(
        split_kernel,
        grid=(2,),
        in_specs=[
            pl.BlockSpec((1, rows, depth), lambda k, e=e: (2 * e + k, 0, 0)) for e in ends
        ],
        out_specs=[pl.BlockSpec((1, rows, depth), lambda k: (k, 0, 0)) for _ in ends],
        out_shape=[jax.ShapeDtypeStruct((2, rows, depth), BF16) for _ in ends],
        name="halves_of",
    )(*stacks)


def kv_kernel(upper_ref, own_ref, other_ref, cos_ref, sin_ref, kv_ref):
    half = DH // 2
    own = own_ref[...].astype(F32)
    other = other_ref[...].astype(F32)
    is_upper = upper_ref[0] == 1
    low = jnp.where(is_upper, other, own)
    high = jnp.where(is_upper, own, other)
    left = lax.broadcasted_iota(jnp.int32, low.shape, 1) < half
    keys = jnp.where(left, low, pltpu.roll(high, half, 1))
    values = jnp.where(left, pltpu.roll(low, half, 1), high)
    keys = keys * cos_ref[...] + pltpu.roll(keys, half, 1) * sin_ref[...]
    kv_ref[:, :DH] = keys.astype(BF16)
    kv_ref[:, DH:] = values.astype(BF16)


def join_kv(upper, own, other, cosine, sine):
    vmem = pl.BlockSpec(memory_space=pltpu.VMEM)
    return pl.pallas_call(
        kv_kernel,
        in_specs=[pl.BlockSpec(memory_space=pltpu.SMEM)] + [vmem] * 4,
        out_specs=vmem,
        out_shape=jax.ShapeDtypeStruct((own.shape[0], 2 * DH), BF16),
        name="join_kv",
    )(upper, own, other, cosine, sine)


def half_ones():
    half = DH // 2
    i0 = lax.broadcasted_iota(jnp.int32, (2 * DH, 2 * DH), 0) // half
    i1 = lax.broadcasted_iota(jnp.int32, (2 * DH, 2 * DH), 1) // half
    return (i0 == i1).astype(F32).astype(BF16)


def half_sums(u, halves):
    return jnp.concatenate(
        [dot(u[:, c : c + 2 * DH], halves) for c in range(0, u.shape[1], 2 * DH)], 1
    )


def wide_map(m_ref, heads):
    highs, lows = [], []
    for h in range(heads):
        w = m_ref[h] * math.log2(math.e)
        w = jnp.concatenate([w, -w], 1)
        high = w.astype(BF16)
        highs.append(high)
        lows.append((w - high.astype(F32)).astype(BF16))
    return jnp.concatenate([jnp.concatenate(highs, 1), jnp.concatenate(lows, 1)], 0)


def features(rows, w, halves):
    e = jnp.exp2(dot(jnp.concatenate([rows, rows], 1), w))
    return (e / half_sums(e.astype(BF16), halves)).astype(BF16)


def query_kernel(q_ref, m_ref, qf_ref):
    halves = half_ones()
    heads = m_ref.shape[0]
    w = wide_map(m_ref, heads)
    for h in range(0, heads, 2):
        for r in range(0, q_ref.shape[0], 256):
            parts = []
            for g in (h, h + 1):
                q = q_ref[r : r + 256, g * DH : (g + 1) * DH]
                logits = dot(jnp.concatenate([q, q], 1), w[:, g * DH : (g + 1) * DH])
                parts.append(jnp.exp2(logits))
            e = jnp.concatenate(parts, 1)
            f = e / dot(e.astype(BF16), halves)
            qf_ref[r : r + 256, h * DH : (h + 2) * DH] = f.astype(BF16)


def query_features(queries, map_query):
    vmem = pl.BlockSpec(memory_space=pltpu.VMEM)
    rows, width = queries.shape
    return pl.pallas_call(
        query_kernel,
        in_specs=[vmem] * 2,
        out_specs=vmem,
        out_shape=jax.ShapeDtypeStruct((rows, width), BF16),
        compiler_params=pltpu.CompilerParams(vmem_limit_bytes=24 * 2**20),
        cost_estimate=pl.CostEstimate(
            flops=rows * width * 1024, bytes_accessed=4 * rows * width, transcendentals=rows * width
        ),
        name="query_features",
    )(queries, map_query)


FOLD = math.log2(math.e) / math.sqrt(DH)


def local_kernel(q_ref, qf_ref, kv_ref, mk_ref, kf_ref, acc_ref, nd_ref, *, tile):
    halves = half_ones()
    rows = q_ref.shape[0]
    heads = mk_ref.shape[0]
    w = wide_map(mk_ref, heads)
    tiles = rows // tile
    for i in range(tiles):
        r = slice(i * tile, (i + 1) * tile)
        kf_ref[r, :] = features(kv_ref[r, :DH], w, halves)
    row_i = lax.broadcasted_iota(jnp.int32, (tile, tile), 0)
    col_i = lax.broadcasted_iota(jnp.int32, (tile, tile), 1)
    lower = col_i <= row_i
    ones = jnp.ones((rows, DH), BF16)
    for i in range(tiles):
        r = slice(i * tile, (i + 1) * tile)
        n = (i + 1) * tile
        va = jnp.concatenate([kv_ref[:n, DH:], ones[:n]], 1)
        for h in range(heads):
            lanes = slice(h * DH, (h + 1) * DH)

            def masked(u):
                last = jnp.where(lower, u[:, n - tile :], 0.0)
                return last if i == 0 else jnp.concatenate([u[:, : n - tile], last], 1)

            p = masked(jnp.exp2(dot(q_ref[r, lanes], kv_ref[:n, :DH], NT) * FOLD))
            acc_ref[h, r, :] = dot(p.astype(BF16), va)
            a = masked(dot(qf_ref[r, lanes], kf_ref[:n, lanes], NT))
            nd_ref[h, r, :] = dot(a.astype(BF16), va)


def local_part(queries, query_feats, kv, map_key, tile=256):
    rows, width = queries.shape
    heads = width // DH
    vmem = pl.BlockSpec(memory_space=pltpu.VMEM)
    wide = jax.ShapeDtypeStruct((heads, rows, 2 * DH), F32)
    return pl.pallas_call(
        functools.partial(local_kernel, tile=tile),
        in_specs=[vmem] * 4,
        out_specs=[vmem] * 3,
        out_shape=[jax.ShapeDtypeStruct((rows, width), BF16), wide, wide],
        compiler_params=pltpu.CompilerParams(vmem_limit_bytes=32 * 2**20),
        cost_estimate=pl.CostEstimate(
            flops=6 * rows * rows * width,
            bytes_accessed=20 * rows * width,
            transcendentals=rows * rows * heads,
        ),
        name="local_part",
    )(queries, query_feats, kv, map_key)


def attention_kernel(
    chain_ref, q_ref, qf_ref, kf_ref, acc_in, nd_in, kv_ref, mate_ref,
    b1_ref, m1_ref, b2_ref, m2_ref, b3_ref, m3_ref, mk_ref,
    out_ref, g_ref,
    kv_s, kf_s, acc_s, nd_s, state_s, state_b, dstate_s, dl_s, gk_s, sems,
    *, tile, head_tile,
):
    core = chain_ref[0] % 2
    chips = chain_ref[0] // 2
    rows = q_ref.shape[0]
    heads = mk_ref.shape[0]
    half = DH // 2
    load_acc = pltpu.make_async_copy(acc_in, acc_s, sems.at[0])
    load_nd = pltpu.make_async_copy(nd_in, nd_s, sems.at[1])
    load_acc.start()
    load_nd.start()
    halves = half_ones()
    pair = halves[:DH, :DH]
    w_key = wide_map(mk_ref, heads)

    for j, ref in enumerate((mate_ref, b1_ref, m1_ref, b2_ref, m2_ref, b3_ref, m3_ref)):

        @pl.when((core == 1) if j == 0 else (chips > (j - 1) // 2))
        def _(j=j, ref=ref):
            kv_s[j * rows : (j + 1) * rows, :] = ref[...]

    state_s[...] = jnp.zeros_like(state_s)
    gk_s[...] = jnp.zeros_like(gk_s)
    ones = jnp.ones((rows, DH), BF16)
    ones_t = jnp.ones((DH, rows), BF16)
    load_acc.wait()
    load_nd.wait()

    def earlier(j, carry):
        first = pl.multiple_of(j * rows, rows)
        for i in range(rows // tile):
            at = pl.multiple_of(first + i * tile, tile)
            kf_s[pl.ds(at, tile), :] = features(kv_s[pl.ds(at, tile), :DH], w_key, halves)
        vat = jnp.concatenate([kv_s[pl.ds(first, rows), DH:].T, ones_t], 0)
        state_s[...] += dot(vat, kf_s[pl.ds(first, rows), :])
        k = kv_s[pl.ds(first, rows), :DH]
        va = jnp.concatenate([kv_s[pl.ds(first, rows), DH:], ones], 1)
        for h in range(heads):
            for i in range(rows // tile):
                r = slice(i * tile, (i + 1) * tile)
                p = jnp.exp2(dot(q_ref[r, h * DH : (h + 1) * DH], k, NT) * FOLD)
                acc_s[h, r, :] += dot(p.astype(BF16), va)
        return carry

    begin = 1 - core
    end = 1 + 2 * chips
    lax.fori_loop(begin, end, earlier, 0)

    state_b[...] = state_s[...].astype(BF16)
    t = head_tile
    tiles = rows // t
    lower = lax.broadcasted_iota(jnp.int32, (t, t), 1) <= lax.broadcasted_iota(
        jnp.int32, (t, t), 0
    )

    def span(i):
        return slice(i * t, (i + 1) * t)

    def head(h, carry):
        lanes = pl.ds(pl.multiple_of(h * DH, DH), DH)
        st = state_b[:, lanes]
        dkf = [None] * tiles
        dst = None
        gq = None
        for i in range(tiles):
            r = span(i)
            qf = qf_ref[r, lanes]
            nd = nd_s[h, r, :] + dot(qf, st, NT)
            inv = 1.0 / nd[:, DH:]
            student = nd[:, :DH] * inv
            out_ref[r, lanes] = student.astype(BF16)
            target = (acc_s[h, r, :DH] / acc_s[h, r, DH:]).astype(BF16).astype(F32)
            g = 2.0 * (student - target) * inv
            gden = -jnp.sum(g * student, -1, keepdims=True) * (1.0 / DH)
            ga = jnp.concatenate([g, jnp.broadcast_to(gden, g.shape)], 1).astype(BF16)
            dqf = dot(ga, st)
            for c in range(i + 1):
                va = jnp.concatenate([kv_ref[span(c), DH:], ones[:t]], 1)
                da = dot(ga, va, NT)
                if c == i:
                    da = jnp.where(lower, da, 0.0)
                da = da.astype(BF16)
                dqf += dot(da, kf_ref[span(c), lanes])
                piece = dot(da, qf, TN)
                dkf[c] = piece if dkf[c] is None else dkf[c] + piece
            piece = dot(ga, qf, TN)
            dst = piece if dst is None else dst + piece
            u = qf.astype(F32) * dqf
            dl = u - qf.astype(F32) * dot(u.astype(BF16), pair)
            piece = dot(q_ref[r, lanes], dl.astype(BF16), TN)
            gq = piece if gq is None else gq + piece
        g_ref[h, :, :half] = gq[:, :half] - gq[:, half:]
        dstate_s[:, lanes] = dst.astype(BF16)
        for c in range(tiles):
            f = kf_ref[span(c), lanes].astype(F32)
            u = f * dkf[c]
            dl = u - f * dot(u.astype(BF16), pair)
            gk_s[:, lanes] += dot(kv_ref[span(c), :DH], dl.astype(BF16), TN)
        return carry

    lax.fori_loop(0, heads, head, 0)

    def earlier_back(j, carry):
        first = pl.multiple_of(j * rows, rows)
        for i in range(rows // tile):
            at = pl.multiple_of(first + i * tile, tile)
            va = jnp.concatenate([kv_s[pl.ds(at, tile), DH:], ones[:tile]], 1)
            f = kf_s[pl.ds(at, tile), :].astype(F32)
            u = f * dot(va, dstate_s[...])
            dl = u - f * half_sums(u.astype(BF16), halves)
            dl_s[i * tile : (i + 1) * tile, :] = dl.astype(BF16)
        gk_s[...] += dot(kv_s[pl.ds(first, rows), :DH].T, dl_s[...])
        return carry

    lax.fori_loop(begin, end, earlier_back, 0)
    for h in range(heads):
        left = gk_s[:, h * DH : h * DH + half]
        g_ref[h, :, half:] = left - gk_s[:, h * DH + half : (h + 1) * DH]


def attention(chain_index, queries, query_feats, local, kv, others, map_key, tile=256, head_tile=768):
    rows, width = queries.shape
    heads = width // DH
    earlier = len(others) * rows
    vmem = pl.BlockSpec(memory_space=pltpu.VMEM)
    held = pl.BlockSpec(memory_space=pl.ANY)
    return pl.pallas_call(
        functools.partial(attention_kernel, tile=tile, head_tile=head_tile),
        in_specs=[pl.BlockSpec(memory_space=pltpu.SMEM)]
        + [vmem] * 3
        + [held] * 2
        + [vmem] * (2 + len(others)),
        out_specs=[vmem] * 2,
        out_shape=[
            jax.ShapeDtypeStruct((rows, width), BF16),
            jax.ShapeDtypeStruct((heads, DH, DH), F32),
        ],
        scratch_shapes=[
            pltpu.VMEM((earlier, 2 * DH), BF16),
            pltpu.VMEM((earlier, width), BF16),
            pltpu.VMEM((heads, rows, 2 * DH), F32),
            pltpu.VMEM((heads, rows, 2 * DH), F32),
            pltpu.VMEM((2 * DH, width), F32),
            pltpu.VMEM((2 * DH, width), BF16),
            pltpu.VMEM((2 * DH, width), BF16),
            pltpu.VMEM((rows, width), BF16),
            pltpu.VMEM((DH, width), F32),
            pltpu.SemaphoreType.DMA((2,)),
        ],
        compiler_params=pltpu.CompilerParams(vmem_limit_bytes=56 * 2**20),
        name="attention",
    )(chain_index, queries, query_feats, *local, kv, *others, map_key)


def hop_x(value, by):
    pairs = [(4 * z + x, 4 * z + (x + by) % 4) for z in range(4) for x in range(4)]
    return lax.ppermute(value, "head", pairs)


def hop_z(value, by):
    pairs = [(4 * z + x, 4 * ((z + by) % 4) + x) for z in range(4) for x in range(4)]
    return lax.ppermute(value, "head", pairs)


def hop_y(value, pairs):
    return lax.ppermute(
        value, "seq", [(2 * a + core, 2 * b + core) for a, b in pairs for core in range(2)]
    )


def per_device(tokens, w_query, w_key, w_value, map_query, map_key):
    row_count, depth = tokens.shape
    half = depth // 2
    chain_index = lax.axis_index("seq")
    place = lax.axis_index("head")
    z, x = place // 4, place % 4
    order = (0, 3, 1, 2)
    xs = [(x + d) % 4 for d in order]
    zs = [(z + d) % 4 for d in order]

    first, second = tokens[:, :half], tokens[:, half:]
    a = [first, hop_x(first, 1), hop_x(first, -1), hop_x(first, 2)]
    b = [second, hop_z(second, 1), hop_z(second, -1), hop_z(second, 2)]
    stack_a, stack_b = jnp.stack(a), jnp.stack(b)
    a_left, a_right = hop_z(stack_a, 1), hop_z(stack_a, -1)
    b_left, b_right = hop_x(stack_b, 1), hop_x(stack_b, -1)

    def at_a(zz, which):
        return [2 * (4 * zz + xs[k]) for k in which]

    def at_b(xx, which):
        return [2 * (4 * zs[k] + xx) + 1 for k in which]

    def table(*parts):
        return jnp.stack([v for p in parts for v in p]).astype(jnp.int32)

    every = range(4)
    w_kv = jnp.concatenate([w_key, w_value], 1)
    cosine, sine = rope_tables(row_count, DH, chain_index * row_count)
    near, away = (0, 1), (2, 3)
    weights = (w_query, w_kv)
    acc = project(table(at_a(z, every), at_b(x, every)), [stack_a, stack_b], weights)
    acc, a_left, a_right, b_left, b_right = lax.optimization_barrier(
        (acc, a_left, a_right, b_left, b_right)
    )
    a0, a1, b0, b1 = halves_of((a_left, a_right, b_left, b_right), (0, 1, 0, 1))
    a0_far, a1_far = hop_z(a0, 1), hop_z(a1, -1)
    b0_far, b1_far = hop_x(b0, 1), hop_x(b1, -1)
    acc_q, acc_kv = project(
        table(
            at_a(zs[1], every), at_a(zs[2], every), at_b(xs[1], every), at_b(xs[2], every)
        ),
        [a_left, a_right, b_left, b_right], weights, acc,
    )
    far_table = table(at_a(zs[3], near), at_a(zs[3], away), at_b(xs[3], near), at_b(xs[3], away))
    far = [a0_far, a1_far, b0_far, b1_far]
    (own,) = project(far_table, far, (w_kv,), (acc_kv,), ())
    other = partner(own, "head", 0)
    (queries,) = project(far_table, far, (w_query,), (acc_q,), (cosine, sine))
    queries, other = lax.optimization_barrier((queries, other))
    upper = jnp.full((1,), place % 2, jnp.int32)
    kv = join_kv(upper, own, other, cosine, sine)

    below = hop_y(kv, [(0, 1), (1, 2), (2, 3)])
    below3 = hop_y(kv, [(0, 3)])
    below2 = hop_y(kv, [(0, 2), (1, 3)])
    mate = partner(kv, "seq", 0)
    query_feats = query_features(queries, map_query)
    local = local_part(queries, query_feats, kv, map_key)
    mate1 = partner(below, "seq", 0)
    mate3 = partner(below3, "seq", 0)
    local, below2 = lax.optimization_barrier((local, below2))
    mate2 = partner(below2, "seq", 0)
    student_out, grads = attention(
        jnp.full((1,), chain_index, jnp.int32), queries, query_feats, local, kv,
        (mate, below, mate1, below2, mate2, below3, mate3), map_key,
    )

    core = chain_index % 2
    mine = grads.shape[0] // 2
    kept = lax.dynamic_slice_in_dim(grads, core * mine, mine, 0)
    given = lax.dynamic_slice_in_dim(grads, (1 - core) * mine, mine, 0)
    kept = kept + partner(given, "seq", 0)
    ahead = hop_y(kept, [(y, (y + 1) % 4) for y in range(4)])
    behind = hop_y(kept, [(y, (y + 3) % 4) for y in range(4)])
    across = hop_y(kept, [(y, (y + 2) % 4) for y in range(4)])
    kept = (kept + across) + (ahead + behind)
    given = partner(kept, "seq", 0)
    grads = jnp.where(
        core == 0, jnp.concatenate([kept, given], 0), jnp.concatenate([given, kept], 0)
    )
    half = DH // 2
    return (student_out, grads[:, :, :half], grads[:, :, half:])


def solution(mesh):
    in_specs = (
        P("seq", "head"),
        P(None, "head"),
        P(None, "head"),
        P(None, "head"),
        P("head", None, None),
        P("head", None, None),
    )
    out_specs = (P("seq", "head"), P("head", None, None), P("head", None, None))
    return jax.shard_map(
        per_device, mesh=mesh, in_specs=in_specs, out_specs=out_specs, check_vma=False
    )
```

```python
import functools
import math

import jax
import jax.numpy as jnp
from jax import lax
from jax.experimental import pallas as pl
from jax.experimental.pallas import tpu as pltpu
from jax.sharding import PartitionSpec as P

DH = 128
ROPE_BASE = 500000.0
NT = (((1,), (1,)), ((), ()))
TN = (((0,), (0,)), ((), ()))
F32 = jnp.float32
BF16 = jnp.bfloat16


def partner(value, axis, apart):
    mask = 2**apart
    pairs = [(source, source ^ mask) for source in range(lax.axis_size(axis))]
    return lax.ppermute(value, axis, pairs)


def rope_tables(length, width, offset):
    half_width = width // 2
    positions = (offset + jnp.arange(length)).astype(F32)
    exponent = jnp.arange(half_width).astype(F32) * (2.0 / width)
    frequency = jnp.power(jnp.float32(ROPE_BASE), -exponent)
    angles = positions[:, None] * frequency[None, :]
    cosine, sine = jnp.cos(angles), jnp.sin(angles)
    return jnp.concatenate([cosine, cosine], 1), jnp.concatenate([-sine, sine], 1)


def dot(a, b, dims=None):
    if dims is None:
        return jnp.dot(a, b, preferred_element_type=F32)
    return lax.dot_general(a, b, dims, preferred_element_type=F32)


def gather_kernel(counts, widths, begin, turned, *refs):
    table_ref = refs[0]
    n, m = len(counts), len(widths)
    x_refs = refs[1 : 1 + n]
    w_refs = refs[1 + n : 1 + n + 2 * m]
    rest = refs[1 + n + 2 * m :]
    if begin:
        ins = rest[:m]
        rest = rest[m:]
    if turned is not None:
        if turned:
            cos_ref, sin_ref = rest[:2]
            rest = rest[2:]
        outs, accs = rest[:m], rest[m:]
    else:
        accs = rest
    step = pl.program_id(0)

    @pl.when(step == 0)
    def _():
        for k in range(m):
            accs[k][...] = ins[k][...] if begin else jnp.zeros_like(accs[k])

    first = 0
    for x_ref, count in zip(x_refs, counts):

        @pl.when((step >= first) & (step < first + count))
        def _():
            for k in range(m):
                accs[k][...] += dot(x_ref[0], w_refs[2 * k][...]) + dot(
                    x_ref[1], w_refs[2 * k + 1][...]
                )

        first += count

    if turned is not None:

        @pl.when(step == pl.num_programs(0) - 1)
        def _():
            for out, acc in zip(outs, accs):
                if turned:
                    for h in range(out.shape[1] // DH):
                        u = acc[:, h * DH : (h + 1) * DH]
                        u = u * cos_ref[...] + pltpu.roll(u, DH // 2, 1) * sin_ref[...]
                        out[:, h * DH : (h + 1) * DH] = u.astype(BF16)
                else:
                    out[...] = acc[...].astype(BF16)


def project(table, stacks, weights, start=None, final=None):
    rows, depth = stacks[0].shape[1:]
    widths = [w.shape[1] for w in weights]
    counts = [s.shape[0] // 2 for s in stacks]
    steps = sum(counts)
    in_specs = []
    first = 0
    for count in counts:
        in_specs.append(
            pl.BlockSpec(
                (2, rows, depth),
                lambda k, t, first=first, count=count: (jnp.clip(k - first, 0, count - 1), 0, 0),
            )
        )
        first += count
    operands = [table, *stacks]
    for w in weights:
        for j in range(2):
            in_specs.append(
                pl.BlockSpec((depth, w.shape[1]), lambda k, t, j=j: (t[2 * k + j], 0))
            )
            operands.append(w)
    whole = [pl.BlockSpec((rows, width), lambda k, t: (0, 0)) for width in widths]
    if start is not None:
        in_specs += whole
        operands += list(start)
    scratch = []
    held = F32
    if final is not None:
        in_specs += [pl.BlockSpec((rows, DH), lambda k, t: (0, 0))] * len(final)
        operands += list(final)
        scratch = [pltpu.VMEM((rows, width), F32) for width in widths]
        held = BF16
    return pl.pallas_call(
        functools.partial(
            gather_kernel, counts, widths, start is not None, None if final is None else bool(final)
        ),
        grid_spec=pltpu.PrefetchScalarGridSpec(
            num_scalar_prefetch=1,
            grid=(steps,),
            in_specs=in_specs,
            out_specs=whole,
            scratch_shapes=scratch,
        ),
        out_shape=[jax.ShapeDtypeStruct((rows, width), held) for width in widths],
        compiler_params=pltpu.CompilerParams(vmem_limit_bytes=40 * 2**20),
        cost_estimate=pl.CostEstimate(
            flops=steps * 4 * rows * depth * sum(widths),
            bytes_accessed=steps * 4 * depth * (rows + sum(widths)),
            transcendentals=0,
        ),
        name="project",
    )(*operands)


def split_kernel(*refs):
    n = len(refs) // 2
    for k in range(n):
        refs[n + k][...] = refs[k][...]


def halves_of(stacks, ends):
    rows, depth = stacks[0].shape[1:]
    return pl.pallas_call(
        split_kernel,
        grid=(2,),
        in_specs=[
            pl.BlockSpec((1, rows, depth), lambda k, e=e: (2 * e + k, 0, 0)) for e in ends
        ],
        out_specs=[pl.BlockSpec((1, rows, depth), lambda k: (k, 0, 0)) for _ in ends],
        out_shape=[jax.ShapeDtypeStruct((2, rows, depth), BF16) for _ in ends],
        name="halves_of",
    )(*stacks)


def kv_kernel(upper_ref, own_ref, other_ref, cos_ref, sin_ref, kv_ref):
    half = DH // 2
    own = own_ref[...].astype(F32)
    other = other_ref[...].astype(F32)
    is_upper = upper_ref[0] == 1
    low = jnp.where(is_upper, other, own)
    high = jnp.where(is_upper, own, other)
    left = lax.broadcasted_iota(jnp.int32, low.shape, 1) < half
    keys = jnp.where(left, low, pltpu.roll(high, half, 1))
    values = jnp.where(left, pltpu.roll(low, half, 1), high)
    keys = keys * cos_ref[...] + pltpu.roll(keys, half, 1) * sin_ref[...]
    kv_ref[:, :DH] = keys.astype(BF16)
    kv_ref[:, DH:] = values.astype(BF16)


def join_kv(upper, own, other, cosine, sine):
    vmem = pl.BlockSpec(memory_space=pltpu.VMEM)
    return pl.pallas_call(
        kv_kernel,
        in_specs=[pl.BlockSpec(memory_space=pltpu.SMEM)] + [vmem] * 4,
        out_specs=vmem,
        out_shape=jax.ShapeDtypeStruct((own.shape[0], 2 * DH), BF16),
        name="join_kv",
    )(upper, own, other, cosine, sine)


def half_ones():
    half = DH // 2
    i0 = lax.broadcasted_iota(jnp.int32, (2 * DH, 2 * DH), 0) // half
    i1 = lax.broadcasted_iota(jnp.int32, (2 * DH, 2 * DH), 1) // half
    return (i0 == i1).astype(F32).astype(BF16)


def half_sums(u, halves):
    return jnp.concatenate(
        [dot(u[:, c : c + 2 * DH], halves) for c in range(0, u.shape[1], 2 * DH)], 1
    )


def wide_map(m_ref, heads):
    highs, lows = [], []
    for h in range(heads):
        w = m_ref[h] * math.log2(math.e)
        w = jnp.concatenate([w, -w], 1)
        high = w.astype(BF16)
        highs.append(high)
        lows.append((w - high.astype(F32)).astype(BF16))
    return jnp.concatenate([jnp.concatenate(highs, 1), jnp.concatenate(lows, 1)], 0)


def features(rows, w, halves):
    e = jnp.exp2(dot(jnp.concatenate([rows, rows], 1), w))
    return (e / half_sums(e.astype(BF16), halves)).astype(BF16)


def feature_kernel(q_ref, kv_ref, mq_ref, mk_ref, qf_ref, kf_ref, mark_ref):
    halves = half_ones()
    heads = mq_ref.shape[0]
    w = wide_map(mq_ref, heads)
    for h in range(0, heads, 2):
        parts = []
        for g in (h, h + 1):
            q = q_ref[:, g * DH : (g + 1) * DH]
            logits = dot(jnp.concatenate([q, q], 1), w[:, g * DH : (g + 1) * DH])
            parts.append(jnp.exp2(logits))
        e = jnp.concatenate(parts, 1)
        f = e / dot(e.astype(BF16), halves)
        qf_ref[:, h * DH : (h + 2) * DH] = f.astype(BF16)
    kf_ref[...] = features(kv_ref[:, :DH], wide_map(mk_ref, heads), halves)
    mark_ref[...] = jnp.zeros_like(mark_ref)


def own_features(queries, kv, map_query, map_key):
    vmem = pl.BlockSpec(memory_space=pltpu.VMEM)
    rows, width = queries.shape
    return pl.pallas_call(
        feature_kernel,
        in_specs=[vmem] * 4,
        out_specs=[vmem] * 3,
        out_shape=[
            jax.ShapeDtypeStruct((rows, width), BF16),
            jax.ShapeDtypeStruct((rows, width), BF16),
            jax.ShapeDtypeStruct((8, DH), F32),
        ],
        compiler_params=pltpu.CompilerParams(vmem_limit_bytes=20 * 2**20),
        cost_estimate=pl.CostEstimate(
            flops=rows * width * 2048,
            bytes_accessed=8 * rows * width,
            transcendentals=2 * rows * width,
        ),
        name="own_features",
    )(queries, kv, map_query, map_key)


FOLD = math.log2(math.e) / math.sqrt(DH)


def attention_kernel(
    chain_ref, q_ref, qf_ref, kf_ref, kv_ref, mate_ref,
    b1_ref, m1_ref, b2_ref, m2_ref, b3_ref, m3_ref, mk_ref, mark_ref,
    out_ref, g_ref,
    kv_s, kf_s, acc_s, nd_s, state_s, state_b, dstate_s, dl_s, gk_s,
    *, tile, head_tile,
):
    core = chain_ref[0] % 2
    chips = chain_ref[0] // 2
    rows = q_ref.shape[0]
    heads = mk_ref.shape[0]
    half = DH // 2
    halves = half_ones()
    pair = halves[:DH, :DH]
    w_key = wide_map(mk_ref, heads)

    for j, ref in enumerate((mate_ref, b1_ref, m1_ref, b2_ref, m2_ref, b3_ref, m3_ref)):

        @pl.when((core == 1) if j == 0 else (chips > (j - 1) // 2))
        def _(j=j, ref=ref):
            kv_s[j * rows : (j + 1) * rows, :] = ref[...]

    state_s[...] = jnp.zeros_like(state_s)
    gk_s[...] = jnp.zeros_like(gk_s)
    ones = jnp.ones((rows, DH), BF16)
    ones_t = jnp.ones((DH, rows), BF16)

    row_i = lax.broadcasted_iota(jnp.int32, (tile, tile), 0)
    diagonal = lax.broadcasted_iota(jnp.int32, (tile, tile), 1) <= row_i
    for i in range(rows // tile):
        r = slice(i * tile, (i + 1) * tile)
        n = (i + 1) * tile
        own = jnp.concatenate([kv_ref[:n, DH:], ones[:n]], 1)

        def masked(u, i=i, n=n):
            last = jnp.where(diagonal, u[:, n - tile :], 0.0)
            return last if i == 0 else jnp.concatenate([u[:, : n - tile], last], 1)

        for h in range(heads):
            lanes = slice(h * DH, (h + 1) * DH)
            p = masked(jnp.exp2(dot(q_ref[r, lanes], kv_ref[:n, :DH], NT) * FOLD))
            acc_s[h, r, :] = dot(p.astype(BF16), own)
            a = masked(dot(qf_ref[r, lanes], kf_ref[:n, lanes], NT))
            nd_s[h, r, :] = dot(a.astype(BF16), own)

    def earlier(j, carry):
        first = pl.multiple_of(j * rows, rows)
        for i in range(rows // 768):
            at = pl.multiple_of(first + i * 768, 768)
            kf_s[pl.ds(at, 768), :] = features(kv_s[pl.ds(at, 768), :DH], w_key, halves)
        vat = jnp.concatenate([kv_s[pl.ds(first, rows), DH:].T, ones_t], 0)
        state_s[...] += dot(vat, kf_s[pl.ds(first, rows), :])
        k = kv_s[pl.ds(first, rows), :DH]
        va = jnp.concatenate([kv_s[pl.ds(first, rows), DH:], ones], 1)
        for h in range(heads):
            for i in range(rows // tile):
                r = slice(i * tile, (i + 1) * tile)
                p = jnp.exp2(dot(q_ref[r, h * DH : (h + 1) * DH], k, NT) * FOLD)
                acc_s[h, r, :] += dot(p.astype(BF16), va)
        return carry

    begin = 1 - core
    end = 1 + 2 * chips
    lax.fori_loop(begin, end, earlier, 0)

    state_b[...] = state_s[...].astype(BF16)
    t = head_tile
    tiles = rows // t
    lower = lax.broadcasted_iota(jnp.int32, (t, t), 1) <= lax.broadcasted_iota(
        jnp.int32, (t, t), 0
    )

    def span(i):
        return slice(i * t, (i + 1) * t)

    def head(h, carry):
        lanes = pl.ds(pl.multiple_of(h * DH, DH), DH)
        st = state_b[:, lanes]
        dkf = [None] * tiles
        dst = None
        gq = None
        for i in range(tiles):
            r = span(i)
            qf = qf_ref[r, lanes]
            nd = nd_s[h, r, :] + dot(qf, st, NT)
            inv = 1.0 / nd[:, DH:]
            student = nd[:, :DH] * inv
            out_ref[r, lanes] = student.astype(BF16)
            target = (acc_s[h, r, :DH] / acc_s[h, r, DH:]).astype(BF16).astype(F32)
            g = 2.0 * (student - target) * inv
            gden = -jnp.sum(g * student, -1, keepdims=True) * (1.0 / DH)
            ga = jnp.concatenate([g, jnp.broadcast_to(gden, g.shape)], 1).astype(BF16)
            dqf = dot(ga, st)
            for c in range(i + 1):
                va = jnp.concatenate([kv_ref[span(c), DH:], ones[:t]], 1)
                da = dot(ga, va, NT)
                if c == i:
                    da = jnp.where(lower, da, 0.0)
                da = da.astype(BF16)
                dqf += dot(da, kf_ref[span(c), lanes])
                piece = dot(da, qf, TN)
                dkf[c] = piece if dkf[c] is None else dkf[c] + piece
            piece = dot(ga, qf, TN)
            dst = piece if dst is None else dst + piece
            u = qf.astype(F32) * dqf
            dl = u - qf.astype(F32) * dot(u.astype(BF16), pair)
            piece = dot(q_ref[r, lanes], dl.astype(BF16), TN)
            gq = piece if gq is None else gq + piece
        g_ref[h, :, :half] = gq[:, :half] - gq[:, half:]
        dstate_s[:, lanes] = dst.astype(BF16)
        for c in range(tiles):
            f = kf_ref[span(c), lanes].astype(F32)
            u = f * dkf[c]
            dl = u - f * dot(u.astype(BF16), pair)
            gk_s[:, lanes] += dot(kv_ref[span(c), :DH], dl.astype(BF16), TN)
        return carry

    lax.fori_loop(0, heads, head, 0, unroll=heads)

    def earlier_back(j, carry):
        first = pl.multiple_of(j * rows, rows)
        for i in range(rows // 768):
            at = pl.multiple_of(first + i * 768, 768)
            va = jnp.concatenate([kv_s[pl.ds(at, 768), DH:], ones[:768]], 1)
            f = kf_s[pl.ds(at, 768), :].astype(F32)
            u = f * dot(va, dstate_s[...])
            dl = u - f * half_sums(u.astype(BF16), halves)
            dl_s[i * 768 : (i + 1) * 768, :] = dl.astype(BF16)
        gk_s[...] += dot(kv_s[pl.ds(first, rows), :DH].T, dl_s[...])
        return carry

    lax.fori_loop(begin, end, earlier_back, 0)
    for h in range(heads):
        left = gk_s[:, h * DH : h * DH + half]
        g_ref[h, :, half:] = left - gk_s[:, h * DH + half : (h + 1) * DH]


def attention(chain_index, queries, query_feats, key_feats, kv, others, map_key, mark, tile=256, head_tile=768):
    rows, width = queries.shape
    heads = width // DH
    earlier = len(others) * rows
    vmem = pl.BlockSpec(memory_space=pltpu.VMEM)
    return pl.pallas_call(
        functools.partial(attention_kernel, tile=tile, head_tile=head_tile),
        in_specs=[pl.BlockSpec(memory_space=pltpu.SMEM)]
        + [vmem] * (6 + len(others)),
        out_specs=[vmem] * 2,
        out_shape=[
            jax.ShapeDtypeStruct((rows, width), BF16),
            jax.ShapeDtypeStruct((heads, DH, DH), F32),
        ],
        scratch_shapes=[
            pltpu.VMEM((earlier, 2 * DH), BF16),
            pltpu.VMEM((earlier, width), BF16),
            pltpu.VMEM((heads, rows, 2 * DH), F32),
            pltpu.VMEM((heads, rows, 2 * DH), F32),
            pltpu.VMEM((2 * DH, width), F32),
            pltpu.VMEM((2 * DH, width), BF16),
            pltpu.VMEM((2 * DH, width), BF16),
            pltpu.VMEM((rows, width), BF16),
            pltpu.VMEM((DH, width), F32),
        ],
        compiler_params=pltpu.CompilerParams(vmem_limit_bytes=36 * 2**20),
        name="attention",
    )(chain_index, queries, query_feats, key_feats, kv, *others, map_key, mark)


def hop_x(value, by):
    pairs = [(4 * z + x, 4 * z + (x + by) % 4) for z in range(4) for x in range(4)]
    return lax.ppermute(value, "head", pairs)


def hop_z(value, by):
    pairs = [(4 * z + x, 4 * ((z + by) % 4) + x) for z in range(4) for x in range(4)]
    return lax.ppermute(value, "head", pairs)


def hop_y(value, pairs):
    return lax.ppermute(
        value, "seq", [(2 * a + core, 2 * b + core) for a, b in pairs for core in range(2)]
    )


def per_device(tokens, w_query, w_key, w_value, map_query, map_key):
    row_count, depth = tokens.shape
    half = depth // 2
    chain_index = lax.axis_index("seq")
    place = lax.axis_index("head")
    z, x = place // 4, place % 4
    order = (0, 3, 1, 2)
    xs = [(x + d) % 4 for d in order]
    zs = [(z + d) % 4 for d in order]

    first, second = tokens[:, :half], tokens[:, half:]
    a = [first, hop_x(first, 1), hop_x(first, -1), hop_x(first, 2)]
    b = [second, hop_z(second, 1), hop_z(second, -1), hop_z(second, 2)]
    stack_a, stack_b = jnp.stack(a), jnp.stack(b)
    a_left, a_right = hop_z(stack_a, 1), hop_z(stack_a, -1)
    b_left, b_right = hop_x(stack_b, 1), hop_x(stack_b, -1)

    def at_a(zz, which):
        return [2 * (4 * zz + xs[k]) for k in which]

    def at_b(xx, which):
        return [2 * (4 * zs[k] + xx) + 1 for k in which]

    def table(*parts):
        return jnp.stack([v for p in parts for v in p]).astype(jnp.int32)

    every = range(4)
    w_kv = jnp.concatenate([w_key, w_value], 1)
    cosine, sine = rope_tables(row_count, DH, chain_index * row_count)
    near, away = (0, 1), (2, 3)
    weights = (w_query, w_kv)
    acc = project(table(at_a(z, every), at_b(x, every)), [stack_a, stack_b], weights)
    acc_q, acc_kv = acc
    acc_kv, a_left, a_right, b_left, b_right = lax.optimization_barrier(
        (acc_kv, a_left, a_right, b_left, b_right)
    )
    a0, a1, b0, b1 = halves_of((a_left, a_right, b_left, b_right), (0, 1, 0, 1))
    a0_far, a1_far = hop_z(a0, 1), hop_z(a1, -1)
    b0_far, b1_far = hop_x(b0, 1), hop_x(b1, -1)
    acc_q, acc_kv = project(
        table(
            at_a(zs[1], every), at_a(zs[2], every), at_b(xs[1], every), at_b(xs[2], every)
        ),
        [a_left, a_right, b_left, b_right], weights, (acc_q, acc_kv),
    )
    far_table = table(at_a(zs[3], near), at_a(zs[3], away), at_b(xs[3], near), at_b(xs[3], away))
    far = [a0_far, a1_far, b0_far, b1_far]
    (own,) = project(far_table, far, (w_kv,), (acc_kv,), ())
    other = partner(own, "head", 0)
    upper = jnp.full((1,), place % 2, jnp.int32)
    kv = join_kv(upper, own, other, cosine, sine)
    last_table, kv = lax.optimization_barrier((far_table, kv))

    below = hop_y(kv, [(0, 1), (1, 2), (2, 3)])
    below3 = hop_y(kv, [(0, 3)])
    below2 = hop_y(kv, [(0, 2), (1, 3)])
    mate = partner(kv, "seq", 0)
    (queries,) = project(last_table, far, (w_query,), (acc_q,), (cosine, sine))
    query_feats, key_feats, mark = own_features(queries, kv, map_query, map_key)
    mate1 = partner(below, "seq", 0)
    mate3 = partner(below3, "seq", 0)
    mark, below2 = lax.optimization_barrier((mark, below2))
    mate2 = partner(below2, "seq", 0)
    student_out, grads = attention(
        jnp.full((1,), chain_index, jnp.int32), queries, query_feats, key_feats, kv,
        (mate, below, mate1, below2, mate2, below3, mate3), map_key, mark,
    )

    core = chain_index % 2
    mine = grads.shape[0] // 2
    kept = lax.dynamic_slice_in_dim(grads, core * mine, mine, 0)
    given = lax.dynamic_slice_in_dim(grads, (1 - core) * mine, mine, 0)
    kept = (kept + partner(given, "seq", 0)).astype(BF16)
    ahead = hop_y(kept, [(y, (y + 1) % 4) for y in range(4)])
    behind = hop_y(kept, [(y, (y + 3) % 4) for y in range(4)])
    across = hop_y(kept, [(y, (y + 2) % 4) for y in range(4)])
    kept, ahead, behind, across = [u.astype(F32) for u in (kept, ahead, behind, across)]
    kept = (kept + across) + (ahead + behind)
    given = partner(kept, "seq", 0)
    grads = jnp.where(
        core == 0, jnp.concatenate([kept, given], 0), jnp.concatenate([given, kept], 0)
    )
    half = DH // 2
    return (student_out, grads[:, :, :half], grads[:, :, half:])


def solution(mesh):
    in_specs = (
        P("seq", "head"),
        P(None, "head"),
        P(None, "head"),
        P(None, "head"),
        P("head", None, None),
        P("head", None, None),
    )
    out_specs = (P("seq", "head"), P("head", None, None), P("head", None, None))
    return jax.shard_map(
        per_device, mesh=mesh, in_specs=in_specs, out_specs=out_specs, check_vma=False
    )
```

```python
import functools
import math

import jax
import jax.numpy as jnp
from jax import lax
from jax.experimental import pallas as pl
from jax.experimental.pallas import tpu as pltpu
from jax.sharding import PartitionSpec as P

DH = 128
ROPE_BASE = 500000.0
NT = (((1,), (1,)), ((), ()))
TN = (((0,), (0,)), ((), ()))
F32 = jnp.float32
BF16 = jnp.bfloat16


def partner(value, axis, apart):
    mask = 2**apart
    pairs = [(source, source ^ mask) for source in range(lax.axis_size(axis))]
    return lax.ppermute(value, axis, pairs)


def rope_tables(length, width, offset):
    half_width = width // 2
    positions = (offset + jnp.arange(length)).astype(F32)
    exponent = jnp.arange(half_width).astype(F32) * (2.0 / width)
    frequency = jnp.power(jnp.float32(ROPE_BASE), -exponent)
    angles = positions[:, None] * frequency[None, :]
    cosine, sine = jnp.cos(angles), jnp.sin(angles)
    return jnp.concatenate([cosine, cosine], 1), jnp.concatenate([-sine, sine], 1)


def dot(a, b, dims=None):
    if dims is None:
        return jnp.dot(a, b, preferred_element_type=F32)
    return lax.dot_general(a, b, dims, preferred_element_type=F32)


def gather_kernel(counts, widths, begin, turned, *refs):
    table_ref = refs[0]
    n, m = len(counts), len(widths)
    x_refs = refs[1 : 1 + n]
    w_refs = refs[1 + n : 1 + n + 2 * m]
    rest = refs[1 + n + 2 * m :]
    if begin:
        ins = rest[:m]
        rest = rest[m:]
    if turned is not None:
        if turned:
            cos_ref, sin_ref = rest[:2]
            rest = rest[2:]
        outs, accs = rest[:m], rest[m:]
    else:
        accs = rest
    step = pl.program_id(0)

    @pl.when(step == 0)
    def _():
        for k in range(m):
            accs[k][...] = ins[k][...] if begin else jnp.zeros_like(accs[k])

    first = 0
    for x_ref, count in zip(x_refs, counts):

        @pl.when((step >= first) & (step < first + count))
        def _():
            for k in range(m):
                accs[k][...] += dot(x_ref[0], w_refs[2 * k][...]) + dot(
                    x_ref[1], w_refs[2 * k + 1][...]
                )

        first += count

    if turned is not None:

        @pl.when(step == pl.num_programs(0) - 1)
        def _():
            for out, acc in zip(outs, accs):
                if turned:
                    for h in range(out.shape[1] // DH):
                        u = acc[:, h * DH : (h + 1) * DH]
                        u = u * cos_ref[...] + pltpu.roll(u, DH // 2, 1) * sin_ref[...]
                        out[:, h * DH : (h + 1) * DH] = u.astype(BF16)
                else:
                    out[...] = acc[...].astype(BF16)


def project(table, stacks, weights, start=None, final=None):
    rows, depth = stacks[0].shape[1:]
    widths = [w.shape[1] for w in weights]
    counts = [s.shape[0] // 2 for s in stacks]
    steps = sum(counts)
    in_specs = []
    first = 0
    for count in counts:
        in_specs.append(
            pl.BlockSpec(
                (2, rows, depth),
                lambda k, t, first=first, count=count: (jnp.clip(k - first, 0, count - 1), 0, 0),
            )
        )
        first += count
    operands = [table, *stacks]
    for w in weights:
        for j in range(2):
            in_specs.append(
                pl.BlockSpec((depth, w.shape[1]), lambda k, t, j=j: (t[2 * k + j], 0))
            )
            operands.append(w)
    whole = [pl.BlockSpec((rows, width), lambda k, t: (0, 0)) for width in widths]
    if start is not None:
        in_specs += whole
        operands += list(start)
    scratch = []
    held = F32
    if final is not None:
        in_specs += [pl.BlockSpec((rows, DH), lambda k, t: (0, 0))] * len(final)
        operands += list(final)
        scratch = [pltpu.VMEM((rows, width), F32) for width in widths]
        held = BF16
    return pl.pallas_call(
        functools.partial(
            gather_kernel, counts, widths, start is not None, None if final is None else bool(final)
        ),
        grid_spec=pltpu.PrefetchScalarGridSpec(
            num_scalar_prefetch=1,
            grid=(steps,),
            in_specs=in_specs,
            out_specs=whole,
            scratch_shapes=scratch,
        ),
        out_shape=[jax.ShapeDtypeStruct((rows, width), held) for width in widths],
        compiler_params=pltpu.CompilerParams(vmem_limit_bytes=40 * 2**20),
        cost_estimate=pl.CostEstimate(
            flops=steps * 4 * rows * depth * sum(widths),
            bytes_accessed=steps * 4 * depth * (rows + sum(widths)),
            transcendentals=0,
        ),
        name="project",
    )(*operands)


def split_kernel(*refs):
    n = len(refs) // 2
    for k in range(n):
        refs[n + k][...] = refs[k][...]


def halves_of(stacks, ends):
    rows, depth = stacks[0].shape[1:]
    return pl.pallas_call(
        split_kernel,
        grid=(2,),
        in_specs=[
            pl.BlockSpec((1, rows, depth), lambda k, e=e: (2 * e + k, 0, 0)) for e in ends
        ],
        out_specs=[pl.BlockSpec((1, rows, depth), lambda k: (k, 0, 0)) for _ in ends],
        out_shape=[jax.ShapeDtypeStruct((2, rows, depth), BF16) for _ in ends],
        name="halves_of",
    )(*stacks)


def kv_kernel(upper_ref, own_ref, other_ref, cos_ref, sin_ref, kv_ref):
    half = DH // 2
    own = own_ref[...].astype(F32)
    other = other_ref[...].astype(F32)
    is_upper = upper_ref[0] == 1
    low = jnp.where(is_upper, other, own)
    high = jnp.where(is_upper, own, other)
    left = lax.broadcasted_iota(jnp.int32, low.shape, 1) < half
    keys = jnp.where(left, low, pltpu.roll(high, half, 1))
    values = jnp.where(left, pltpu.roll(low, half, 1), high)
    keys = keys * cos_ref[...] + pltpu.roll(keys, half, 1) * sin_ref[...]
    kv_ref[:, :DH] = keys.astype(BF16)
    kv_ref[:, DH:] = values.astype(BF16)


def join_kv(upper, own, other, cosine, sine):
    vmem = pl.BlockSpec(memory_space=pltpu.VMEM)
    return pl.pallas_call(
        kv_kernel,
        in_specs=[pl.BlockSpec(memory_space=pltpu.SMEM)] + [vmem] * 4,
        out_specs=vmem,
        out_shape=jax.ShapeDtypeStruct((own.shape[0], 2 * DH), BF16),
        name="join_kv",
    )(upper, own, other, cosine, sine)


def half_ones():
    half = DH // 2
    i0 = lax.broadcasted_iota(jnp.int32, (2 * DH, 2 * DH), 0) // half
    i1 = lax.broadcasted_iota(jnp.int32, (2 * DH, 2 * DH), 1) // half
    return (i0 == i1).astype(F32).astype(BF16)


def half_sums(u, halves):
    return jnp.concatenate(
        [dot(u[:, c : c + 2 * DH], halves) for c in range(0, u.shape[1], 2 * DH)], 1
    )


def wide_map(m_ref, heads):
    highs, lows = [], []
    for h in range(heads):
        w = m_ref[h] * math.log2(math.e)
        w = jnp.concatenate([w, -w], 1)
        high = w.astype(BF16)
        highs.append(high)
        lows.append((w - high.astype(F32)).astype(BF16))
    return jnp.concatenate([jnp.concatenate(highs, 1), jnp.concatenate(lows, 1)], 0)


def features(rows, w, halves):
    e = jnp.exp2(dot(jnp.concatenate([rows, rows], 1), w))
    return (e / half_sums(e.astype(BF16), halves)).astype(BF16)


def feature_kernel(q_ref, kv_ref, mq_ref, mk_ref, qf_ref, kf_ref, mark_ref):
    halves = half_ones()
    heads = mq_ref.shape[0]
    w = wide_map(mq_ref, heads)
    for h in range(0, heads, 2):
        parts = []
        for g in (h, h + 1):
            q = q_ref[:, g * DH : (g + 1) * DH]
            logits = dot(jnp.concatenate([q, q], 1), w[:, g * DH : (g + 1) * DH])
            parts.append(jnp.exp2(logits))
        e = jnp.concatenate(parts, 1)
        f = e / dot(e.astype(BF16), halves)
        qf_ref[:, h * DH : (h + 2) * DH] = f.astype(BF16)
    kf_ref[...] = features(kv_ref[:, :DH], wide_map(mk_ref, heads), halves)
    mark_ref[...] = jnp.zeros_like(mark_ref)


def own_features(queries, kv, map_query, map_key):
    vmem = pl.BlockSpec(memory_space=pltpu.VMEM)
    rows, width = queries.shape
    return pl.pallas_call(
        feature_kernel,
        in_specs=[vmem] * 4,
        out_specs=[vmem] * 3,
        out_shape=[
            jax.ShapeDtypeStruct((rows, width), BF16),
            jax.ShapeDtypeStruct((rows, width), BF16),
            jax.ShapeDtypeStruct((8, DH), F32),
        ],
        compiler_params=pltpu.CompilerParams(vmem_limit_bytes=20 * 2**20),
        cost_estimate=pl.CostEstimate(
            flops=rows * width * 2048,
            bytes_accessed=8 * rows * width,
            transcendentals=2 * rows * width,
        ),
        name="own_features",
    )(queries, kv, map_query, map_key)


FOLD = math.log2(math.e) / math.sqrt(DH)


def attention_kernel(
    chain_ref, q_ref, qf_ref, kf_ref, kv_ref, mate_ref,
    b1_ref, m1_ref, b2_ref, m2_ref, b3_ref, m3_ref, mk_ref, mark_ref,
    out_ref, g_ref,
    kv_s, kf_s, acc_s, nd_s, state_s, state_b, dstate_s, dl_s, gk_s, sems,
    *, tile, head_tile,
):
    core = chain_ref[0] % 2
    chips = chain_ref[0] // 2
    rows = q_ref.shape[0]
    heads = mk_ref.shape[0]
    half = DH // 2
    halves = half_ones()
    pair = halves[:DH, :DH]
    w_key = wide_map(mk_ref, heads)

    loads = []
    for j, ref in enumerate((mate_ref, b1_ref, m1_ref, b2_ref, m2_ref, b3_ref, m3_ref)):
        loads.append(
            pltpu.make_async_copy(ref, kv_s.at[j * rows : (j + 1) * rows, :], sems.at[j])
        )
        loads[-1].start()
    state_s[...] = jnp.zeros_like(state_s)
    gk_s[...] = jnp.zeros_like(gk_s)
    ones = jnp.ones((rows, DH), BF16)
    ones_t = jnp.ones((DH, rows), BF16)

    row_i = lax.broadcasted_iota(jnp.int32, (tile, tile), 0)
    diagonal = lax.broadcasted_iota(jnp.int32, (tile, tile), 1) <= row_i
    for i in range(rows // tile):
        r = slice(i * tile, (i + 1) * tile)
        n = (i + 1) * tile
        own = jnp.concatenate([kv_ref[:n, DH:], ones[:n]], 1)

        def masked(u, i=i, n=n):
            last = jnp.where(diagonal, u[:, n - tile :], 0.0)
            return last if i == 0 else jnp.concatenate([u[:, : n - tile], last], 1)

        for h in range(heads):
            lanes = slice(h * DH, (h + 1) * DH)
            p = masked(jnp.exp2(dot(q_ref[r, lanes], kv_ref[:n, :DH], NT) * FOLD))
            acc_s[h, r, :] = dot(p.astype(BF16), own)
            a = masked(dot(qf_ref[r, lanes], kf_ref[:n, lanes], NT))
            nd_s[h, r, :] = dot(a.astype(BF16), own)

    for load in loads:
        load.wait()

    def earlier(j, carry):
        first = pl.multiple_of(j * rows, rows)
        for i in range(rows // 768):
            at = pl.multiple_of(first + i * 768, 768)
            kf_s[pl.ds(at, 768), :] = features(kv_s[pl.ds(at, 768), :DH], w_key, halves)
        vat = jnp.concatenate([kv_s[pl.ds(first, rows), DH:].T, ones_t], 0)
        state_s[...] += dot(vat, kf_s[pl.ds(first, rows), :])
        k = kv_s[pl.ds(first, rows), :DH]
        va = jnp.concatenate([kv_s[pl.ds(first, rows), DH:], ones], 1)
        for h in range(heads):
            for i in range(rows // tile):
                r = slice(i * tile, (i + 1) * tile)
                p = jnp.exp2(dot(q_ref[r, h * DH : (h + 1) * DH], k, NT) * FOLD)
                acc_s[h, r, :] += dot(p.astype(BF16), va)
        return carry

    begin = 1 - core
    end = 1 + 2 * chips
    lax.fori_loop(begin, end, earlier, 0)

    state_b[...] = state_s[...].astype(BF16)
    t = head_tile
    tiles = rows // t
    lower = lax.broadcasted_iota(jnp.int32, (t, t), 1) <= lax.broadcasted_iota(
        jnp.int32, (t, t), 0
    )

    def span(i):
        return slice(i * t, (i + 1) * t)

    def head(h, carry):
        lanes = pl.ds(pl.multiple_of(h * DH, DH), DH)
        st = state_b[:, lanes]
        dkf = [None] * tiles
        dst = None
        gq = None
        for i in range(tiles):
            r = span(i)
            qf = qf_ref[r, lanes]
            nd = nd_s[h, r, :] + dot(qf, st, NT)
            inv = 1.0 / nd[:, DH:]
            student = nd[:, :DH] * inv
            out_ref[r, lanes] = student.astype(BF16)
            target = (acc_s[h, r, :DH] / acc_s[h, r, DH:]).astype(BF16).astype(F32)
            g = 2.0 * (student - target) * inv
            gden = -jnp.sum(g * student, -1, keepdims=True) * (1.0 / DH)
            ga = jnp.concatenate([g, jnp.broadcast_to(gden, g.shape)], 1).astype(BF16)
            dqf = dot(ga, st)
            for c in range(i + 1):
                va = jnp.concatenate([kv_ref[span(c), DH:], ones[:t]], 1)
                da = dot(ga, va, NT)
                if c == i:
                    da = jnp.where(lower, da, 0.0)
                da = da.astype(BF16)
                dqf += dot(da, kf_ref[span(c), lanes])
                piece = dot(da, qf, TN)
                dkf[c] = piece if dkf[c] is None else dkf[c] + piece
            piece = dot(ga, qf, TN)
            dst = piece if dst is None else dst + piece
            u = qf.astype(F32) * dqf
            dl = u - qf.astype(F32) * dot(u.astype(BF16), pair)
            piece = dot(q_ref[r, lanes], dl.astype(BF16), TN)
            gq = piece if gq is None else gq + piece
        g_ref[h, :, :half] = gq[:, :half] - gq[:, half:]
        dstate_s[:, lanes] = dst.astype(BF16)
        for c in range(tiles):
            f = kf_ref[span(c), lanes].astype(F32)
            u = f * dkf[c]
            dl = u - f * dot(u.astype(BF16), pair)
            gk_s[:, lanes] += dot(kv_ref[span(c), :DH], dl.astype(BF16), TN)
        return carry

    lax.fori_loop(0, heads, head, 0, unroll=heads)

    def earlier_back(j, carry):
        first = pl.multiple_of(j * rows, rows)
        for i in range(rows // 768):
            at = pl.multiple_of(first + i * 768, 768)
            va = jnp.concatenate([kv_s[pl.ds(at, 768), DH:], ones[:768]], 1)
            f = kf_s[pl.ds(at, 768), :].astype(F32)
            u = f * dot(va, dstate_s[...])
            dl = u - f * half_sums(u.astype(BF16), halves)
            dl_s[i * 768 : (i + 1) * 768, :] = dl.astype(BF16)
        gk_s[...] += dot(kv_s[pl.ds(first, rows), :DH].T, dl_s[...])
        return carry

    lax.fori_loop(begin, end, earlier_back, 0)
    for h in range(heads):
        left = gk_s[:, h * DH : h * DH + half]
        g_ref[h, :, half:] = left - gk_s[:, h * DH + half : (h + 1) * DH]


def attention(chain_index, queries, query_feats, key_feats, kv, others, map_key, mark, tile=256, head_tile=768):
    rows, width = queries.shape
    heads = width // DH
    earlier = len(others) * rows
    vmem = pl.BlockSpec(memory_space=pltpu.VMEM)
    return pl.pallas_call(
        functools.partial(attention_kernel, tile=tile, head_tile=head_tile),
        in_specs=[pl.BlockSpec(memory_space=pltpu.SMEM)]
        + [vmem] * 4
        + [pl.BlockSpec(memory_space=pl.ANY)] * len(others)
        + [vmem] * 2,
        out_specs=[vmem] * 2,
        out_shape=[
            jax.ShapeDtypeStruct((rows, width), BF16),
            jax.ShapeDtypeStruct((heads, DH, DH), F32),
        ],
        scratch_shapes=[
            pltpu.VMEM((earlier, 2 * DH), BF16),
            pltpu.VMEM((earlier, width), BF16),
            pltpu.VMEM((heads, rows, 2 * DH), F32),
            pltpu.VMEM((heads, rows, 2 * DH), F32),
            pltpu.VMEM((2 * DH, width), F32),
            pltpu.VMEM((2 * DH, width), BF16),
            pltpu.VMEM((2 * DH, width), BF16),
            pltpu.VMEM((rows, width), BF16),
            pltpu.VMEM((DH, width), F32),
            pltpu.SemaphoreType.DMA((len(others),)),
        ],
        compiler_params=pltpu.CompilerParams(vmem_limit_bytes=36 * 2**20),
        name="attention",
    )(chain_index, queries, query_feats, key_feats, kv, *others, map_key, mark)


def hop_x(value, by):
    pairs = [(4 * z + x, 4 * z + (x + by) % 4) for z in range(4) for x in range(4)]
    return lax.ppermute(value, "head", pairs)


def hop_z(value, by):
    pairs = [(4 * z + x, 4 * ((z + by) % 4) + x) for z in range(4) for x in range(4)]
    return lax.ppermute(value, "head", pairs)


def hop_y(value, pairs):
    return lax.ppermute(
        value, "seq", [(2 * a + core, 2 * b + core) for a, b in pairs for core in range(2)]
    )


def per_device(tokens, w_query, w_key, w_value, map_query, map_key):
    row_count, depth = tokens.shape
    half = depth // 2
    chain_index = lax.axis_index("seq")
    place = lax.axis_index("head")
    z, x = place // 4, place % 4
    order = (0, 3, 1, 2)
    xs = [(x + d) % 4 for d in order]
    zs = [(z + d) % 4 for d in order]

    first, second = tokens[:, :half], tokens[:, half:]
    a = [first, hop_x(first, 1), hop_x(first, -1), hop_x(first, 2)]
    b = [second, hop_z(second, 1), hop_z(second, -1), hop_z(second, 2)]
    stack_a, stack_b = jnp.stack(a), jnp.stack(b)
    a_left, a_right = hop_z(stack_a, 1), hop_z(stack_a, -1)
    b_left, b_right = hop_x(stack_b, 1), hop_x(stack_b, -1)

    def at_a(zz, which):
        return [2 * (4 * zz + xs[k]) for k in which]

    def at_b(xx, which):
        return [2 * (4 * zs[k] + xx) + 1 for k in which]

    def table(*parts):
        return jnp.stack([v for p in parts for v in p]).astype(jnp.int32)

    every = range(4)
    w_kv = jnp.concatenate([w_key, w_value], 1)
    cosine, sine = rope_tables(row_count, DH, chain_index * row_count)
    near, away = (0, 1), (2, 3)
    weights = (w_query, w_kv)
    acc = project(table(at_a(z, every), at_b(x, every)), [stack_a, stack_b], weights)
    acc_q, acc_kv = acc
    acc_kv, a_left, a_right, b_left, b_right = lax.optimization_barrier(
        (acc_kv, a_left, a_right, b_left, b_right)
    )
    a0, a1, b0, b1 = halves_of((a_left, a_right, b_left, b_right), (0, 1, 0, 1))
    a0_far, a1_far = hop_z(a0, 1), hop_z(a1, -1)
    b0_far, b1_far = hop_x(b0, 1), hop_x(b1, -1)
    acc_q, acc_kv = project(
        table(
            at_a(zs[1], every), at_a(zs[2], every), at_b(xs[1], every), at_b(xs[2], every)
        ),
        [a_left, a_right, b_left, b_right], weights, (acc_q, acc_kv),
    )
    far_table = table(at_a(zs[3], near), at_a(zs[3], away), at_b(xs[3], near), at_b(xs[3], away))
    far = [a0_far, a1_far, b0_far, b1_far]
    (own,) = project(far_table, far, (w_kv,), (acc_kv,), ())
    other = partner(own, "head", 0)
    upper = jnp.full((1,), place % 2, jnp.int32)
    kv = join_kv(upper, own, other, cosine, sine)
    last_table, kv = lax.optimization_barrier((far_table, kv))

    below = hop_y(kv, [(0, 1), (1, 2), (2, 3)])
    below3 = hop_y(kv, [(0, 3)])
    below2 = hop_y(kv, [(0, 2), (1, 3)])
    mate = partner(kv, "seq", 0)
    (queries,) = project(last_table, far, (w_query,), (acc_q,), (cosine, sine))
    query_feats, key_feats, mark = own_features(queries, kv, map_query, map_key)
    mate1 = partner(below, "seq", 0)
    mate3 = partner(below3, "seq", 0)
    mark, below2 = lax.optimization_barrier((mark, below2))
    mate2 = partner(below2, "seq", 0)
    student_out, grads = attention(
        jnp.full((1,), chain_index, jnp.int32), queries, query_feats, key_feats, kv,
        (mate, below, mate1, below2, mate2, below3, mate3), map_key, mark,
    )

    core = chain_index % 2
    mine = grads.shape[0] // 2
    kept = lax.dynamic_slice_in_dim(grads, core * mine, mine, 0)
    given = lax.dynamic_slice_in_dim(grads, (1 - core) * mine, mine, 0)
    kept = (kept + partner(given, "seq", 0)).astype(BF16)
    ahead = hop_y(kept, [(y, (y + 1) % 4) for y in range(4)])
    behind = hop_y(kept, [(y, (y + 3) % 4) for y in range(4)])
    across = hop_y(kept, [(y, (y + 2) % 4) for y in range(4)])
    kept, ahead, behind, across = [u.astype(F32) for u in (kept, ahead, behind, across)]
    kept = (kept + across) + (ahead + behind)
    given = partner(kept, "seq", 0)
    grads = jnp.where(
        core == 0, jnp.concatenate([kept, given], 0), jnp.concatenate([given, kept], 0)
    )
    half = DH // 2
    return (student_out, grads[:, :, :half], grads[:, :, half:])


def solution(mesh):
    in_specs = (
        P("seq", "head"),
        P(None, "head"),
        P(None, "head"),
        P(None, "head"),
        P("head", None, None),
        P("head", None, None),
    )
    out_specs = (P("seq", "head"), P("head", None, None), P("head", None, None))
    return jax.shard_map(
        per_device, mesh=mesh, in_specs=in_specs, out_specs=out_specs, check_vma=False
    )
```

```python
import functools
import math

import jax
import jax.numpy as jnp
from jax import lax
from jax.experimental import pallas as pl
from jax.experimental.pallas import tpu as pltpu
from jax.sharding import PartitionSpec as P

DH = 128
ROPE_BASE = 500000.0
NT = (((1,), (1,)), ((), ()))
TN = (((0,), (0,)), ((), ()))
F32 = jnp.float32
BF16 = jnp.bfloat16


def partner(value, axis, apart):
    mask = 2**apart
    pairs = [(source, source ^ mask) for source in range(lax.axis_size(axis))]
    return lax.ppermute(value, axis, pairs)


def rope_tables(length, width, offset):
    half_width = width // 2
    positions = (offset + jnp.arange(length)).astype(F32)
    exponent = jnp.arange(half_width).astype(F32) * (2.0 / width)
    frequency = jnp.power(jnp.float32(ROPE_BASE), -exponent)
    angles = positions[:, None] * frequency[None, :]
    cosine, sine = jnp.cos(angles), jnp.sin(angles)
    return jnp.concatenate([cosine, cosine], 1), jnp.concatenate([-sine, sine], 1)


def dot(a, b, dims=None):
    if dims is None:
        return jnp.dot(a, b, preferred_element_type=F32)
    return lax.dot_general(a, b, dims, preferred_element_type=F32)


def gather_kernel(counts, widths, begin, turned, *refs):
    table_ref = refs[0]
    n, m = len(counts), len(widths)
    x_refs = refs[1 : 1 + n]
    w_refs = refs[1 + n : 1 + n + 2 * m]
    rest = refs[1 + n + 2 * m :]
    if begin:
        ins = rest[:m]
        rest = rest[m:]
    if turned is not None:
        if turned:
            cos_ref, sin_ref = rest[:2]
            rest = rest[2:]
        outs, accs = rest[:m], rest[m:]
    else:
        accs = rest
    step = pl.program_id(0)

    @pl.when(step == 0)
    def _():
        for k in range(m):
            accs[k][...] = ins[k][...] if begin else jnp.zeros_like(accs[k])

    first = 0
    for x_ref, count in zip(x_refs, counts):

        @pl.when((step >= first) & (step < first + count))
        def _():
            for k in range(m):
                accs[k][...] += dot(x_ref[0], w_refs[2 * k][...]) + dot(
                    x_ref[1], w_refs[2 * k + 1][...]
                )

        first += count

    if turned is not None:

        @pl.when(step == pl.num_programs(0) - 1)
        def _():
            for out, acc in zip(outs, accs):
                if turned:
                    for h in range(out.shape[1] // DH):
                        u = acc[:, h * DH : (h + 1) * DH]
                        u = u * cos_ref[...] + pltpu.roll(u, DH // 2, 1) * sin_ref[...]
                        out[:, h * DH : (h + 1) * DH] = u.astype(BF16)
                else:
                    out[...] = acc[...].astype(BF16)


def project(table, stacks, weights, start=None, final=None):
    rows, depth = stacks[0].shape[1:]
    widths = [w.shape[1] for w in weights]
    counts = [s.shape[0] // 2 for s in stacks]
    steps = sum(counts)
    in_specs = []
    first = 0
    for count in counts:
        in_specs.append(
            pl.BlockSpec(
                (2, rows, depth),
                lambda k, t, first=first, count=count: (jnp.clip(k - first, 0, count - 1), 0, 0),
            )
        )
        first += count
    operands = [table, *stacks]
    for w in weights:
        for j in range(2):
            in_specs.append(
                pl.BlockSpec((depth, w.shape[1]), lambda k, t, j=j: (t[2 * k + j], 0))
            )
            operands.append(w)
    whole = [pl.BlockSpec((rows, width), lambda k, t: (0, 0)) for width in widths]
    if start is not None:
        in_specs += whole
        operands += list(start)
    scratch = []
    held = F32
    if final is not None:
        in_specs += [pl.BlockSpec((rows, DH), lambda k, t: (0, 0))] * len(final)
        operands += list(final)
        scratch = [pltpu.VMEM((rows, width), F32) for width in widths]
        held = BF16
    return pl.pallas_call(
        functools.partial(
            gather_kernel, counts, widths, start is not None, None if final is None else bool(final)
        ),
        grid_spec=pltpu.PrefetchScalarGridSpec(
            num_scalar_prefetch=1,
            grid=(steps,),
            in_specs=in_specs,
            out_specs=whole,
            scratch_shapes=scratch,
        ),
        out_shape=[jax.ShapeDtypeStruct((rows, width), held) for width in widths],
        compiler_params=pltpu.CompilerParams(vmem_limit_bytes=40 * 2**20),
        cost_estimate=pl.CostEstimate(
            flops=steps * 4 * rows * depth * sum(widths),
            bytes_accessed=steps * 4 * depth * (rows + sum(widths)),
            transcendentals=0,
        ),
        name="project",
    )(*operands)


def split_kernel(ends, *refs):
    n = len(ends)
    held, sems = refs[2 * n :]
    loads = [
        pltpu.make_async_copy(refs[k].at[2 * e : 2 * e + 2], held.at[k], sems.at[0, k])
        for k, e in enumerate(ends)
    ]
    stores = [
        pltpu.make_async_copy(held.at[k], refs[n + k], sems.at[1, k]) for k in range(n)
    ]
    for load in loads:
        load.start()
    for load, store in zip(loads, stores):
        load.wait()
        store.start()
    for store in stores:
        store.wait()


def halves_of(stacks, ends):
    rows, depth = stacks[0].shape[1:]
    held = pl.BlockSpec(memory_space=pl.ANY)
    return pl.pallas_call(
        functools.partial(split_kernel, ends),
        in_specs=[held] * len(ends),
        out_specs=[held] * len(ends),
        out_shape=[jax.ShapeDtypeStruct((2, rows, depth), BF16) for _ in ends],
        scratch_shapes=[
            pltpu.VMEM((len(ends), 2, rows, depth), BF16),
            pltpu.SemaphoreType.DMA((2, len(ends))),
        ],
        compiler_params=pltpu.CompilerParams(vmem_limit_bytes=52 * 2**20),
        name="halves_of",
    )(*stacks)


def kv_kernel(upper_ref, own_ref, other_ref, cos_ref, sin_ref, kv_ref):
    half = DH // 2
    own = own_ref[...].astype(F32)
    other = other_ref[...].astype(F32)
    is_upper = upper_ref[0] == 1
    low = jnp.where(is_upper, other, own)
    high = jnp.where(is_upper, own, other)
    left = lax.broadcasted_iota(jnp.int32, low.shape, 1) < half
    keys = jnp.where(left, low, pltpu.roll(high, half, 1))
    values = jnp.where(left, pltpu.roll(low, half, 1), high)
    keys = keys * cos_ref[...] + pltpu.roll(keys, half, 1) * sin_ref[...]
    kv_ref[:, :DH] = keys.astype(BF16)
    kv_ref[:, DH:] = values.astype(BF16)


def join_kv(upper, own, other, cosine, sine):
    vmem = pl.BlockSpec(memory_space=pltpu.VMEM)
    return pl.pallas_call(
        kv_kernel,
        in_specs=[pl.BlockSpec(memory_space=pltpu.SMEM)] + [vmem] * 4,
        out_specs=vmem,
        out_shape=jax.ShapeDtypeStruct((own.shape[0], 2 * DH), BF16),
        name="join_kv",
    )(upper, own, other, cosine, sine)


def half_ones():
    half = DH // 2
    i0 = lax.broadcasted_iota(jnp.int32, (2 * DH, 2 * DH), 0) // half
    i1 = lax.broadcasted_iota(jnp.int32, (2 * DH, 2 * DH), 1) // half
    return (i0 == i1).astype(F32).astype(BF16)


def half_sums(u, halves):
    return jnp.concatenate(
        [dot(u[:, c : c + 2 * DH], halves) for c in range(0, u.shape[1], 2 * DH)], 1
    )


def wide_map(m_ref, heads):
    highs, lows = [], []
    for h in range(heads):
        w = m_ref[h] * math.log2(math.e)
        w = jnp.concatenate([w, -w], 1)
        high = w.astype(BF16)
        highs.append(high)
        lows.append((w - high.astype(F32)).astype(BF16))
    return jnp.concatenate([jnp.concatenate(highs, 1), jnp.concatenate(lows, 1)], 0)


def features(rows, w, halves):
    e = jnp.exp2(dot(jnp.concatenate([rows, rows], 1), w))
    return (e / half_sums(e.astype(BF16), halves)).astype(BF16)


def feature_kernel(q_ref, kv_ref, mq_ref, mk_ref, qf_ref, kf_ref, mark_ref):
    halves = half_ones()
    heads = mq_ref.shape[0]
    w = wide_map(mq_ref, heads)
    for h in range(0, heads, 2):
        parts = []
        for g in (h, h + 1):
            q = q_ref[:, g * DH : (g + 1) * DH]
            logits = dot(jnp.concatenate([q, q], 1), w[:, g * DH : (g + 1) * DH])
            parts.append(jnp.exp2(logits))
        e = jnp.concatenate(parts, 1)
        f = e / dot(e.astype(BF16), halves)
        qf_ref[:, h * DH : (h + 2) * DH] = f.astype(BF16)
    kf_ref[...] = features(kv_ref[:, :DH], wide_map(mk_ref, heads), halves)
    mark_ref[...] = jnp.zeros_like(mark_ref)


def own_features(queries, kv, map_query, map_key):
    vmem = pl.BlockSpec(memory_space=pltpu.VMEM)
    rows, width = queries.shape
    return pl.pallas_call(
        feature_kernel,
        in_specs=[vmem] * 4,
        out_specs=[vmem] * 3,
        out_shape=[
            jax.ShapeDtypeStruct((rows, width), BF16),
            jax.ShapeDtypeStruct((rows, width), BF16),
            jax.ShapeDtypeStruct((8, DH), F32),
        ],
        compiler_params=pltpu.CompilerParams(vmem_limit_bytes=20 * 2**20),
        cost_estimate=pl.CostEstimate(
            flops=rows * width * 2048,
            bytes_accessed=8 * rows * width,
            transcendentals=2 * rows * width,
        ),
        name="own_features",
    )(queries, kv, map_query, map_key)


FOLD = math.log2(math.e) / math.sqrt(DH)


def attention_kernel(
    chain_ref, q_ref, qf_ref, kf_ref, kv_ref, mate_ref,
    b1_ref, m1_ref, b2_ref, m2_ref, b3_ref, m3_ref, mk_ref, mark_ref,
    out_ref, kept_ref, given_ref,
    kv_s, kf_s, acc_s, nd_s, state_s, state_b, dstate_s, dl_s, gk_s, g_ref, sems,
    *, tile, head_tile,
):
    core = chain_ref[0] % 2
    chips = chain_ref[0] // 2
    rows = q_ref.shape[0]
    heads = mk_ref.shape[0]
    half = DH // 2
    halves = half_ones()
    pair = halves[:DH, :DH]
    w_key = wide_map(mk_ref, heads)

    loads = []
    for j, ref in enumerate((mate_ref, b1_ref, m1_ref, b2_ref, m2_ref, b3_ref, m3_ref)):
        loads.append(
            pltpu.make_async_copy(ref, kv_s.at[j * rows : (j + 1) * rows, :], sems.at[j])
        )
        loads[-1].start()
    state_s[...] = jnp.zeros_like(state_s)
    gk_s[...] = jnp.zeros_like(gk_s)
    ones = jnp.ones((rows, DH), BF16)
    ones_t = jnp.ones((DH, rows), BF16)

    row_i = lax.broadcasted_iota(jnp.int32, (tile, tile), 0)
    diagonal = lax.broadcasted_iota(jnp.int32, (tile, tile), 1) <= row_i
    for i in range(rows // tile):
        r = slice(i * tile, (i + 1) * tile)
        n = (i + 1) * tile
        own = jnp.concatenate([kv_ref[:n, DH:], ones[:n]], 1)

        def masked(u, i=i, n=n):
            last = jnp.where(diagonal, u[:, n - tile :], 0.0)
            return last if i == 0 else jnp.concatenate([u[:, : n - tile], last], 1)

        for h in range(heads):
            lanes = slice(h * DH, (h + 1) * DH)
            p = masked(jnp.exp2(dot(q_ref[r, lanes], kv_ref[:n, :DH], NT) * FOLD))
            acc_s[h, r, :] = dot(p.astype(BF16), own)
            a = masked(dot(qf_ref[r, lanes], kf_ref[:n, lanes], NT))
            nd_s[h, r, :] = dot(a.astype(BF16), own)

    for load in loads:
        load.wait()

    def earlier(j, carry):
        first = pl.multiple_of(j * rows, rows)
        for i in range(rows // 768):
            at = pl.multiple_of(first + i * 768, 768)
            kf_s[pl.ds(at, 768), :] = features(kv_s[pl.ds(at, 768), :DH], w_key, halves)
        vat = jnp.concatenate([kv_s[pl.ds(first, rows), DH:].T, ones_t], 0)
        state_s[...] += dot(vat, kf_s[pl.ds(first, rows), :])
        k = kv_s[pl.ds(first, rows), :DH]
        va = jnp.concatenate([kv_s[pl.ds(first, rows), DH:], ones], 1)
        for h in range(heads):
            for i in range(rows // tile):
                r = slice(i * tile, (i + 1) * tile)
                p = jnp.exp2(dot(q_ref[r, h * DH : (h + 1) * DH], k, NT) * FOLD)
                acc_s[h, r, :] += dot(p.astype(BF16), va)
        return carry

    begin = 1 - core
    end = 1 + 2 * chips
    lax.fori_loop(begin, end, earlier, 0)

    state_b[...] = state_s[...].astype(BF16)
    t = head_tile
    tiles = rows // t
    lower = lax.broadcasted_iota(jnp.int32, (t, t), 1) <= lax.broadcasted_iota(
        jnp.int32, (t, t), 0
    )

    def span(i):
        return slice(i * t, (i + 1) * t)

    def head(h, carry):
        lanes = pl.ds(pl.multiple_of(h * DH, DH), DH)
        st = state_b[:, lanes]
        dkf = [None] * tiles
        dst = None
        gq = None
        for i in range(tiles):
            r = span(i)
            qf = qf_ref[r, lanes]
            nd = nd_s[h, r, :] + dot(qf, st, NT)
            inv = 1.0 / nd[:, DH:]
            student = nd[:, :DH] * inv
            out_ref[r, lanes] = student.astype(BF16)
            target = (acc_s[h, r, :DH] / acc_s[h, r, DH:]).astype(BF16).astype(F32)
            g = 2.0 * (student - target) * inv
            gden = -jnp.sum(g * student, -1, keepdims=True) * (1.0 / DH)
            ga = jnp.concatenate([g, jnp.broadcast_to(gden, g.shape)], 1).astype(BF16)
            dqf = dot(ga, st)
            for c in range(i + 1):
                va = jnp.concatenate([kv_ref[span(c), DH:], ones[:t]], 1)
                da = dot(ga, va, NT)
                if c == i:
                    da = jnp.where(lower, da, 0.0)
                da = da.astype(BF16)
                dqf += dot(da, kf_ref[span(c), lanes])
                piece = dot(da, qf, TN)
                dkf[c] = piece if dkf[c] is None else dkf[c] + piece
            piece = dot(ga, qf, TN)
            dst = piece if dst is None else dst + piece
            u = qf.astype(F32) * dqf
            dl = u - qf.astype(F32) * dot(u.astype(BF16), pair)
            piece = dot(q_ref[r, lanes], dl.astype(BF16), TN)
            gq = piece if gq is None else gq + piece
        g_ref[h, :, :half] = gq[:, :half] - gq[:, half:]
        dstate_s[:, lanes] = dst.astype(BF16)
        for c in range(tiles):
            f = kf_ref[span(c), lanes].astype(F32)
            u = f * dkf[c]
            dl = u - f * dot(u.astype(BF16), pair)
            gk_s[:, lanes] += dot(kv_ref[span(c), :DH], dl.astype(BF16), TN)
        return carry

    lax.fori_loop(0, heads, head, 0, unroll=heads)

    def earlier_back(j, carry):
        first = pl.multiple_of(j * rows, rows)
        for i in range(rows // 768):
            at = pl.multiple_of(first + i * 768, 768)
            va = jnp.concatenate([kv_s[pl.ds(at, 768), DH:], ones[:768]], 1)
            f = kf_s[pl.ds(at, 768), :].astype(F32)
            u = f * dot(va, dstate_s[...])
            dl = u - f * half_sums(u.astype(BF16), halves)
            dl_s[i * 768 : (i + 1) * 768, :] = dl.astype(BF16)
        gk_s[...] += dot(kv_s[pl.ds(first, rows), :DH].T, dl_s[...])
        return carry

    lax.fori_loop(begin, end, earlier_back, 0)
    for h in range(heads):
        left = gk_s[:, h * DH : h * DH + half]
        g_ref[h, :, half:] = left - gk_s[:, h * DH + half : (h + 1) * DH]
    mine = heads // 2
    kept_ref[...] = g_ref[pl.ds(core * mine, mine)]
    given_ref[...] = g_ref[pl.ds((1 - core) * mine, mine)]


def attention(chain_index, queries, query_feats, key_feats, kv, others, map_key, mark, tile=256, head_tile=768):
    rows, width = queries.shape
    heads = width // DH
    earlier = len(others) * rows
    vmem = pl.BlockSpec(memory_space=pltpu.VMEM)
    return pl.pallas_call(
        functools.partial(attention_kernel, tile=tile, head_tile=head_tile),
        in_specs=[pl.BlockSpec(memory_space=pltpu.SMEM)]
        + [vmem] * 4
        + [pl.BlockSpec(memory_space=pl.ANY)] * len(others)
        + [vmem] * 2,
        out_specs=[vmem] * 3,
        out_shape=[
            jax.ShapeDtypeStruct((rows, width), BF16),
            jax.ShapeDtypeStruct((heads // 2, DH, DH), F32),
            jax.ShapeDtypeStruct((heads // 2, DH, DH), F32),
        ],
        scratch_shapes=[
            pltpu.VMEM((earlier, 2 * DH), BF16),
            pltpu.VMEM((earlier, width), BF16),
            pltpu.VMEM((heads, rows, 2 * DH), F32),
            pltpu.VMEM((heads, rows, 2 * DH), F32),
            pltpu.VMEM((2 * DH, width), F32),
            pltpu.VMEM((2 * DH, width), BF16),
            pltpu.VMEM((2 * DH, width), BF16),
            pltpu.VMEM((rows, width), BF16),
            pltpu.VMEM((DH, width), F32),
            pltpu.VMEM((heads, DH, DH), F32),
            pltpu.SemaphoreType.DMA((len(others),)),
        ],
        compiler_params=pltpu.CompilerParams(vmem_limit_bytes=36 * 2**20),
        name="attention",
    )(chain_index, queries, query_feats, key_feats, kv, *others, map_key, mark)


def hop_x(value, by):
    pairs = [(4 * z + x, 4 * z + (x + by) % 4) for z in range(4) for x in range(4)]
    return lax.ppermute(value, "head", pairs)


def hop_z(value, by):
    pairs = [(4 * z + x, 4 * ((z + by) % 4) + x) for z in range(4) for x in range(4)]
    return lax.ppermute(value, "head", pairs)


def hop_y(value, pairs):
    return lax.ppermute(
        value, "seq", [(2 * a + core, 2 * b + core) for a, b in pairs for core in range(2)]
    )


def per_device(tokens, w_query, w_key, w_value, map_query, map_key):
    row_count, depth = tokens.shape
    half = depth // 2
    chain_index = lax.axis_index("seq")
    place = lax.axis_index("head")
    z, x = place // 4, place % 4
    order = (0, 3, 1, 2)
    xs = [(x + d) % 4 for d in order]
    zs = [(z + d) % 4 for d in order]

    first, second = tokens[:, :half], tokens[:, half:]
    a = [first, hop_x(first, 1), hop_x(first, -1), hop_x(first, 2)]
    b = [second, hop_z(second, 1), hop_z(second, -1), hop_z(second, 2)]
    stack_a, stack_b = jnp.stack(a), jnp.stack(b)
    a_left, a_right = hop_z(stack_a, 1), hop_z(stack_a, -1)
    b_left, b_right = hop_x(stack_b, 1), hop_x(stack_b, -1)

    def at_a(zz, which):
        return [2 * (4 * zz + xs[k]) for k in which]

    def at_b(xx, which):
        return [2 * (4 * zs[k] + xx) + 1 for k in which]

    def table(*parts):
        return jnp.stack([v for p in parts for v in p]).astype(jnp.int32)

    every = range(4)
    w_kv = jnp.concatenate([w_key, w_value], 1)
    cosine, sine = rope_tables(row_count, DH, chain_index * row_count)
    near, away = (0, 1), (2, 3)
    weights = (w_query, w_kv)
    acc = project(table(at_a(z, every), at_b(x, every)), [stack_a, stack_b], weights)
    acc_q, acc_kv = acc
    acc_kv, a_left, a_right, b_left, b_right = lax.optimization_barrier(
        (acc_kv, a_left, a_right, b_left, b_right)
    )
    a0, a1, b0, b1 = halves_of((a_left, a_right, b_left, b_right), (0, 1, 0, 1))
    a0_far, a1_far = hop_z(a0, 1), hop_z(a1, -1)
    b0_far, b1_far = hop_x(b0, 1), hop_x(b1, -1)
    acc_q, acc_kv = project(
        table(
            at_a(zs[1], every), at_a(zs[2], every), at_b(xs[1], every), at_b(xs[2], every)
        ),
        [a_left, a_right, b_left, b_right], weights, (acc_q, acc_kv),
    )
    far_table = table(at_a(zs[3], near), at_a(zs[3], away), at_b(xs[3], near), at_b(xs[3], away))
    far = [a0_far, a1_far, b0_far, b1_far]
    (own,) = project(far_table, far, (w_kv,), (acc_kv,), ())
    other = partner(own, "head", 0)
    upper = jnp.full((1,), place % 2, jnp.int32)
    kv = join_kv(upper, own, other, cosine, sine)
    last_table, kv = lax.optimization_barrier((far_table, kv))

    below = hop_y(kv, [(0, 1), (1, 2), (2, 3)])
    below3 = hop_y(kv, [(0, 3)])
    below2 = hop_y(kv, [(0, 2), (1, 3)])
    mate = partner(kv, "seq", 0)
    (queries,) = project(last_table, far, (w_query,), (acc_q,), (cosine, sine))
    query_feats, key_feats, mark = own_features(queries, kv, map_query, map_key)
    mate1 = partner(below, "seq", 0)
    mate3 = partner(below3, "seq", 0)
    mark, below2 = lax.optimization_barrier((mark, below2))
    mate2 = partner(below2, "seq", 0)
    student_out, kept, given = attention(
        jnp.full((1,), chain_index, jnp.int32), queries, query_feats, key_feats, kv,
        (mate, below, mate1, below2, mate2, below3, mate3), map_key, mark,
    )

    core = chain_index % 2
    kept = (kept + partner(given, "seq", 0)).astype(BF16)
    ahead = hop_y(kept, [(y, (y + 1) % 4) for y in range(4)])
    behind = hop_y(kept, [(y, (y + 3) % 4) for y in range(4)])
    across = hop_y(kept, [(y, (y + 2) % 4) for y in range(4)])
    kept, ahead, behind, across = [u.astype(F32) for u in (kept, ahead, behind, across)]
    kept = (kept + across) + (ahead + behind)
    given = partner(kept, "seq", 0)
    grads = jnp.where(
        core == 0, jnp.concatenate([kept, given], 0), jnp.concatenate([given, kept], 0)
    )
    half = DH // 2
    return (student_out, grads[:, :, :half], grads[:, :, half:])


def solution(mesh):
    in_specs = (
        P("seq", "head"),
        P(None, "head"),
        P(None, "head"),
        P(None, "head"),
        P("head", None, None),
        P("head", None, None),
    )
    out_specs = (P("seq", "head"), P("head", None, None), P("head", None, None))
    return jax.shard_map(
        per_device, mesh=mesh, in_specs=in_specs, out_specs=out_specs, check_vma=False
    )
```
